32 devices in a mesh: dp: 16 (over z, y, x), tensor: 2 (over core).
Axes of the slice: x: 2, y: 2, z: 4, core: 2. Of those that a mesh axis runs over, the one named last changes fastest.
Arguments:
- source_ids: int32 [16, 512], P('dp', 'tensor'), may hold values from 0 to 50303
- target_ids: int32 [16, 512], P('dp', 'tensor'), may hold values from 0 to 50303
- score_places: int32 [16, 64], P('dp', 'tensor'), may hold values from 0 to 511
- target_labels: int32 [16, 64], P('dp', 'tensor'), may hold values from 0 to 50303
- source_lengths: int32 [16], P('dp'), may hold values from 1 to 512, 4608 in all
- target_lengths: int32 [16], P('dp'), may hold values from 1 to 512, 4608 in all
- pair_order: int32 [16], replicated, may hold values from 0 to 15, each once
- step_count: int32 [1], replicated, may hold values from 1 to 20
- entry_weight: float32 [3, 3, 768, 768], P(None, None, 'dp', 'tensor'), may hold values from -0.21875 to 0.21875
- entry_first: float32 [3, 3, 768, 768], P(None, None, 'dp', 'tensor'), may hold values from -1.9073486e-06 to 1.9073486e-06
- entry_second: float32 [3, 3, 768, 768], P(None, None, 'dp', 'tensor'), may hold values from 8.938092e-16 to 1.4300947e-14
- exit_weight: float32 [3, 768, 768], P(None, 'tensor', 'dp'), may hold values from -0.875 to 0.875
- exit_first: float32 [3, 768, 768], P(None, 'tensor', 'dp'), may hold values from -1.9073486e-06 to 1.9073486e-06
- exit_second: float32 [3, 768, 768], P(None, 'tensor', 'dp'), may hold values from 8.938092e-16 to 1.4300947e-14
- expand_weight: float32 [2, 768, 3072], P(None, 'dp', 'tensor'), may hold values from -0.21875 to 0.21875
- expand_first: float32 [2, 768, 3072], P(None, 'dp', 'tensor'), may hold values from -1.9073486e-06 to 1.9073486e-06
- expand_second: float32 [2, 768, 3072], P(None, 'dp', 'tensor'), may hold values from 8.938092e-16 to 1.4300947e-14
- reduce_weight: float32 [2, 3072, 768], P(None, 'tensor', 'dp'), may hold values from -0.109375 to 0.109375
- reduce_first: float32 [2, 3072, 768], P(None, 'tensor', 'dp'), may hold values from -1.9073486e-06 to 1.9073486e-06
- reduce_second: float32 [2, 3072, 768], P(None, 'tensor', 'dp'), may hold values from 8.938092e-16 to 1.4300947e-14
- norm_gains: float32 [7, 768], replicated, may hold values from 0.5 to 1.5
- gains_first: float32 [7, 768], replicated, may hold values from -2.2888184e-05 to 2.2888184e-05
- gains_second: float32 [7, 768], replicated, may hold values from 8.9380916e-14 to 1.4300946e-12
- token_table: float32 [50304, 768], P(('dp', 'tensor')), may hold values from -1 to 1
- table_first: float32 [50304, 768], P(('dp', 'tensor')), may hold values from -1.9073486e-06 to 1.9073486e-06
- table_second: float32 [50304, 768], P(('dp', 'tensor')), may hold values from 8.938092e-16 to 1.4300947e-14
- place_table: float32 [2, 512, 768], P(None, 'tensor', 'dp'), may hold values from -1 to 1
- place_first: float32 [2, 512, 768], P(None, 'tensor', 'dp'), may hold values from -1.9073486e-06 to 1.9073486e-06
- place_second: float32 [2, 512, 768], P(None, 'tensor', 'dp'), may hold values from 8.938092e-16 to 1.4300947e-14
Outputs:
- mean_loss: float32 [], replicated
- gradient_norm: float32 [], replicated
- pair_losses: float32 [16, 64], P('dp', 'tensor')
- entry_new: float32 [3, 3, 768, 768], P(None, None, 'dp', 'tensor')
- entry_first_new: float32 [3, 3, 768, 768], P(None, None, 'dp', 'tensor')
- entry_second_new: float32 [3, 3, 768, 768], P(None, None, 'dp', 'tensor')
- exit_new: float32 [3, 768, 768], P(None, 'tensor', 'dp')
- exit_first_new: float32 [3, 768, 768], P(None, 'tensor', 'dp')
- exit_second_new: float32 [3, 768, 768], P(None, 'tensor', 'dp')
- expand_new: float32 [2, 768, 3072], P(None, 'dp', 'tensor')
- expand_first_new: float32 [2, 768, 3072], P(None, 'dp', 'tensor')
- expand_second_new: float32 [2, 768, 3072], P(None, 'dp', 'tensor')
- reduce_new: float32 [2, 3072, 768], P(None, 'tensor', 'dp')
- reduce_first_new: float32 [2, 3072, 768], P(None, 'tensor', 'dp')
- reduce_second_new: float32 [2, 3072, 768], P(None, 'tensor', 'dp')
- gains_new: float32 [7, 768], replicated
- gains_first_new: float32 [7, 768], replicated
- gains_second_new: float32 [7, 768], replicated
- table_new: float32 [50304, 768], P(('dp', 'tensor'))
- table_first_new: float32 [50304, 768], P(('dp', 'tensor'))
- table_second_new: float32 [50304, 768], P(('dp', 'tensor'))
- place_new: float32 [2, 512, 768], P(None, 'tensor', 'dp')
- place_first_new: float32 [2, 512, 768], P(None, 'tensor', 'dp')
- place_second_new: float32 [2, 512, 768], P(None, 'tensor', 'dp')
The draws below stay inside these ranges and needn't reach their ends.
Inputs may be any that keep to these rules, and one draw needn't show every extreme that they name: `score_places`: places may repeat; a place counts only where it is below its pair's target length. `source_lengths`: some pair has exactly 512. `target_lengths`: some pair has exactly 512. `pair_order`: each data group index once.
All inputs are finite; a program needn't handle non-finite values. No bound on the sum of `source_lengths` or of `target_lengths` on one device may be relied on, other than what follows from the above.
Results may differ from the reference program's by a relative error of at most 0.012.
The reference program's roundings to bfloat16 on the way count: a program that leaves them out, or rounds other values in their place, can miss the bound.
Values may be sent and summed in bfloat16 or wider, within the bound.
No kernel may reach another device: no remote copies, remote signals or barrier semaphores. Data moves between devices by JAX's collectives and lax.ppermute only.
A program may use at most 384 MiB of HBM per device.

```python
import math
import jax
import jax.numpy as jnp
import numpy as np
from jax import lax

D = 768
HEADS = 12
HEAD_DIM = 64
FF = 3072
VOCAB = 50304
SEQ = 512
SCORED = 64
PAIRS = 16
NPARAM = 55940352


def place_ends(values, key, smallest, largest):
    shape = values.shape
    spot = [jax.random.randint(jax.random.fold_in(key, axis), (), 0, shape[axis]) for axis in range(len(shape))]
    values = values.at[tuple(spot)].set(smallest)
    longest = shape.index(max(shape))
    spot[longest] = (spot[longest] + 1) % shape[longest]
    return values.at[tuple(spot)].set(largest)


def shard_levels(rng, extent, split, least, high):
    def one(dim, parts):
        draws = jax.random.uniform(jax.random.fold_in(jax.random.fold_in(rng, 6), dim), (parts,), jnp.float32, least / len(split), high / len(split))
        return jnp.repeat(jnp.exp(draws), extent[dim] // parts).reshape((-1,) + (1,) * (len(extent) - dim - 1))

    level = one(*split[0])
    for cut in split[1:]:
        level = level * one(*cut)
    return level


def rank_bounds(number_of, lean):
    weights = [(1 << 20) // math.isqrt(grade ** lean) + 1 for grade in range(1, number_of + 1)]
    spread = 1 + sum(weights) // (1 << 30)
    return np.cumsum(np.array([max(1, weight // spread) for weight in weights]))


def ranked_ids(stream_key, dims, count, lean):
    table = rank_bounds(count, lean)
    ticket = jax.random.randint(jax.random.fold_in(stream_key, 1), dims, 0, int(table[count - 1]))
    standing = jnp.searchsorted(jnp.asarray(table, jnp.int32), ticket, side="right")
    return jax.random.permutation(jax.random.fold_in(stream_key, 2), count)[standing].astype(jnp.int32)


def profile(count, total, limit, lean):
    portions = [(1 << 20) // math.isqrt(standing ** lean) + 1 for standing in range(2, count + 1)]
    surplus, holding = total - limit - (count - 1), [1] * (count - 1)
    while surplus > 0:
        free = [i for i in range(count - 1) if holding[i] < limit]
        whole, budget = sum([portions[i] for i in free]), surplus
        for i in free:
            addition = min(limit - holding[i], max(1, budget * portions[i] // whole), surplus)
            holding[i] = holding[i] + addition
            surplus = surplus - addition
    return np.array([limit] + holding)


def ragged(key, number_of, total, reach, skew):
    if number_of == 2:
        one = jax.random.randint(key, (), max(1, total - reach), min(reach, total - 1) + 1)
        return jnp.stack([one, total - one])
    sizes = jnp.asarray(profile(number_of, total, reach, skew), jnp.int32)
    couples = (number_of - 1) // 2
    giver, sink = sizes[1:1 + 2 * couples:2], sizes[2:2 + 2 * couples:2]
    margin = jnp.minimum(giver - 1, reach - sink)
    moved = jax.random.randint(jax.random.fold_in(key, 1), (couples,), 0, 1 << 20) % (margin + 1)
    sizes = sizes.at[1:1 + 2 * couples:2].set(giver - moved).at[2:2 + 2 * couples:2].set(sink + moved)
    return sizes[jax.random.permutation(jax.random.fold_in(key, 2), number_of)]


def scatter_about(key, extent, width, limit, split=(), dtype=jnp.bfloat16):
    entries = width * jax.random.normal(key, extent, jnp.float32)
    if split:
        entries = entries * shard_levels(key, extent, split, -0.22, 0.18)
    return jnp.clip(entries, -limit, limit).astype(dtype)


def setup_inputs(seed: int = 0) -> dict:
    key_list = jax.random.split(jax.random.key(seed), 30)
    source_ids = place_ends(ranked_ids(key_list[0], (PAIRS, SEQ), VOCAB, 2), jax.random.fold_in(key_list[0], 3), 0, VOCAB - 1).astype(jnp.int32)
    target_ids = place_ends(ranked_ids(key_list[1], (PAIRS, SEQ), VOCAB, 2), jax.random.fold_in(key_list[1], 3), 0, VOCAB - 1).astype(jnp.int32)
    score_places = place_ends(jax.random.randint(key_list[2], (PAIRS, SCORED), 0, SEQ), jax.random.fold_in(key_list[2], 1), 0, SEQ - 1).astype(jnp.int32)
    target_labels = place_ends(ranked_ids(key_list[3], (PAIRS, SCORED), VOCAB, 2), jax.random.fold_in(key_list[3], 3), 0, VOCAB - 1).astype(jnp.int32)
    source_lengths = ragged(key_list[4], PAIRS, PAIRS * SEQ * 9 // 16, SEQ, 2).astype(jnp.int32)
    target_lengths = ragged(key_list[5], PAIRS, PAIRS * SEQ * 9 // 16, SEQ, 2).astype(jnp.int32)
    pair_order = jax.random.permutation(key_list[6], PAIRS).astype(jnp.int32)
    step_count = jax.random.randint(key_list[7], (1,), 1, 21).astype(jnp.int32)
    entry_weight = scatter_about(key_list[8], (3, 3, D, D), D ** -0.5, 0.21875, ((2, 16), (3, 2)), jnp.float32)
    entry_first = scatter_about(key_list[9], (3, 3, D, D), (0.00111 * NPARAM ** -0.5), 1.9073486328125e-06, ((2, 16), (3, 2)), jnp.float32)
    entry_second = jnp.clip(jnp.exp(math.log(1.4300946833537866e-14) - 2.7725887 * jax.random.uniform(key_list[10], (3, 3, D, D), jnp.float32) ** shard_levels(key_list[10], (3, 3, D, D), ((2, 16), (3, 2)), -0.2, 0.2)), 8.938091770961166e-16, 1.4300946833537866e-14)
    exit_weight = scatter_about(key_list[11], (3, D, D), (D // 16) ** -0.5, 0.875, ((1, 2), (2, 16)), jnp.float32)
    exit_first = scatter_about(key_list[12], (3, D, D), (0.00111 * NPARAM ** -0.5), 1.9073486328125e-06, ((1, 2), (2, 16)), jnp.float32)
    exit_second = jnp.clip(jnp.exp(math.log(1.4300946833537866e-14) - 2.7725887 * jax.random.uniform(key_list[13], (3, D, D), jnp.float32) ** shard_levels(key_list[13], (3, D, D), ((1, 2), (2, 16)), -0.2, 0.2)), 8.938091770961166e-16, 1.4300946833537866e-14)
    expand_weight = scatter_about(key_list[14], (2, D, FF), D ** -0.5, 0.21875, ((1, 16), (2, 2)), jnp.float32)
    expand_first = scatter_about(key_list[15], (2, D, FF), (0.00111 * NPARAM ** -0.5), 1.9073486328125e-06, ((1, 16), (2, 2)), jnp.float32)
    expand_second = jnp.clip(jnp.exp(math.log(1.4300946833537866e-14) - 2.7725887 * jax.random.uniform(key_list[16], (2, D, FF), jnp.float32) ** shard_levels(key_list[16], (2, D, FF), ((1, 16), (2, 2)), -0.2, 0.2)), 8.938091770961166e-16, 1.4300946833537866e-14)
    reduce_weight = scatter_about(key_list[17], (2, FF, D), FF ** -0.5, 0.109375, ((1, 2), (2, 16)), jnp.float32)
    reduce_first = scatter_about(key_list[18], (2, FF, D), (0.00111 * NPARAM ** -0.5), 1.9073486328125e-06, ((1, 2), (2, 16)), jnp.float32)
    reduce_second = jnp.clip(jnp.exp(math.log(1.4300946833537866e-14) - 2.7725887 * jax.random.uniform(key_list[19], (2, FF, D), jnp.float32) ** shard_levels(key_list[19], (2, FF, D), ((1, 2), (2, 16)), -0.2, 0.2)), 8.938091770961166e-16, 1.4300946833537866e-14)
    norm_gains = jnp.clip(1.0 + 0.1 * jax.random.normal(key_list[20], (7, D), jnp.float32), 0.5, 1.5)
    gains_first = scatter_about(key_list[21], (7, D), (0.0111 * NPARAM ** -0.5), 2.288818359375e-05, (), jnp.float32)
    gains_second = jnp.clip(jnp.exp(jax.random.uniform(key_list[22], (7, D), jnp.float32, math.log(8.938091559202929e-14), math.log(1.4300946494724687e-12))), 8.938091559202929e-14, 1.4300946494724687e-12)
    token_table = scatter_about(key_list[23], (VOCAB, D), (2.0 * D ** -0.5), 1.0, ((0, 32),), jnp.float32)
    table_first = scatter_about(key_list[24], (VOCAB, D), (0.00111 * NPARAM ** -0.5), 1.9073486328125e-06, ((0, 32),), jnp.float32)
    table_second = jnp.clip(jnp.exp(math.log(1.4300946833537866e-14) - 2.7725887 * jax.random.uniform(key_list[25], (VOCAB, D), jnp.float32) ** shard_levels(key_list[25], (VOCAB, D), ((0, 32),), -0.2, 0.2)), 8.938091770961166e-16, 1.4300946833537866e-14)
    place_table = scatter_about(key_list[26], (2, SEQ, D), 0.07, 1.0, ((1, 2), (2, 16)), jnp.float32)
    place_first = scatter_about(key_list[27], (2, SEQ, D), (0.00111 * NPARAM ** -0.5), 1.9073486328125e-06, ((1, 2), (2, 16)), jnp.float32)
    place_second = jnp.clip(jnp.exp(math.log(1.4300946833537866e-14) - 2.7725887 * jax.random.uniform(key_list[28], (2, SEQ, D), jnp.float32) ** shard_levels(key_list[28], (2, SEQ, D), ((1, 2), (2, 16)), -0.2, 0.2)), 8.938091770961166e-16, 1.4300946833537866e-14)
    return dict(source_ids=source_ids, target_ids=target_ids, score_places=score_places, target_labels=target_labels, source_lengths=source_lengths, target_lengths=target_lengths, pair_order=pair_order, step_count=step_count, entry_weight=entry_weight, entry_first=entry_first, entry_second=entry_second, exit_weight=exit_weight, exit_first=exit_first, exit_second=exit_second, expand_weight=expand_weight, expand_first=expand_first, expand_second=expand_second, reduce_weight=reduce_weight, reduce_first=reduce_first, reduce_second=reduce_second, norm_gains=norm_gains, gains_first=gains_first, gains_second=gains_second, token_table=token_table, table_first=table_first, table_second=table_second, place_table=place_table, place_first=place_first, place_second=place_second)


HIGHEST = lax.Precision.HIGHEST
MAX_NORM = 0.01
LEARN_RATE = 0.03
GAIN_RATE = 0.3
FIRST_DECAY = 0.9
SECOND_DECAY = 0.999
ADAM_EPSILON = 1e-08
WEIGHT_DECAY = 0.01

@jax.custom_vjp
def low(v):
    return lax.optimization_barrier(v.astype(jnp.bfloat16)).astype(jnp.float32)

@jax.custom_vjp
def low_back(v):
    return v

def low_keep(v):
    return (low(v), None)

def low_pass(kept, grad):
    return (grad,)

def back_keep(v):
    return (v, None)

def back_low(kept, grad):
    return (low(grad),)
low.defvjp(low_keep, low_pass)
low_back.defvjp(back_keep, back_low)

def rounded(value):
    return low_back(low(value))

def norm_rows(values, gain):
    centered = values - lax.optimization_barrier(jnp.mean(values, axis=-1, keepdims=True))
    variance = lax.optimization_barrier(jnp.mean(centered * centered, axis=-1, keepdims=True))
    return centered * lax.rsqrt(variance + 1e-05) * gain

def matmul(left, right):
    return jnp.dot(left, right, precision=HIGHEST, preferred_element_type=jnp.float32)

def attend(query, key, value, allowed):
    length = query.shape[0]
    keys = key.shape[0]
    query_heads = query.reshape(length, HEADS, HEAD_DIM)
    key_heads = key.reshape(keys, HEADS, HEAD_DIM)
    value_heads = value.reshape(keys, HEADS, HEAD_DIM)
    raw_scores = low_back(jnp.einsum('qhd,khd->hqk', query_heads, key_heads, precision=HIGHEST))
    scores = jnp.where(allowed[None], raw_scores * HEAD_DIM ** (-0.5), -1000000000.0)
    weights = low(jax.nn.softmax(scores, axis=-1))
    mixed = jnp.einsum('hqk,khd->qhd', weights, value_heads, precision=HIGHEST)
    return rounded(mixed.reshape(length, HEADS * HEAD_DIM))

def attention_block(stream, gain, entry, leave, allowed, memory):
    normed = low(norm_rows(stream, gain))
    source = normed if memory is None else memory
    query = rounded(matmul(normed, entry[0]))
    key = rounded(matmul(source, entry[1]))
    value = rounded(matmul(source, entry[2]))
    return low_back(matmul(attend(query, key, value, allowed), leave))

def feed_block(stream, gain, expand, shrink):
    normed = low(norm_rows(stream, gain))
    inner = low_back(matmul(normed, expand))
    hidden = rounded(jax.nn.gelu(inner, approximate=False))
    return low_back(matmul(hidden, shrink))

def pair_loss(used, item, count):
    entry, leave, expand, shrink, gains, table, places = used
    source, target, spots, labels, source_len, target_len = item
    columns = jnp.arange(SEQ)
    enc_allowed = jnp.broadcast_to(columns[None, :] < source_len, (SEQ, SEQ))
    dec_allowed = (columns[None, :] <= columns[:, None]) & (columns[None, :] < target_len)
    stream = low_back(table[source] + places[0])
    stream = stream + attention_block(stream, gains[0], entry[0], leave[0], enc_allowed, None)
    stream = stream + feed_block(stream, gains[1], expand[0], shrink[0])
    memory = low(norm_rows(stream, gains[2]))
    decoded = low_back(table[target] + places[1])
    decoded = decoded + attention_block(decoded, gains[3], entry[1], leave[1], dec_allowed, None)
    decoded = decoded + attention_block(decoded, gains[4], entry[2], leave[2], enc_allowed, memory)
    decoded = decoded + feed_block(decoded, gains[5], expand[1], shrink[1])
    final = low(norm_rows(decoded, gains[6]))
    picked = final[spots]
    logits = low_back(jnp.dot(picked, table.T, precision=HIGHEST))
    total = jax.nn.logsumexp(logits, axis=-1)
    golden = jnp.take_along_axis(logits, labels[:, None], axis=1)[:, 0]
    losses = (total - golden) * (spots < target_len).astype(jnp.float32)
    return (jnp.sum(losses) / count, losses)

def adam_step(master, first, second, grad, clip, fix_one, fix_two, rate):
    grad = grad * clip
    first_new = FIRST_DECAY * first + (1 - FIRST_DECAY) * grad
    second_new = SECOND_DECAY * second + (1 - SECOND_DECAY) * grad * grad
    master_new = master - rate * (first_new / fix_one / (jnp.sqrt(second_new / fix_two) + ADAM_EPSILON) + WEIGHT_DECAY * master)
    return (master_new, first_new, second_new)

def reference(source_ids, target_ids, score_places, target_labels, source_lengths, target_lengths, pair_order, step_count, entry_weight, entry_first, entry_second, exit_weight, exit_first, exit_second, expand_weight, expand_first, expand_second, reduce_weight, reduce_first, reduce_second, norm_gains, gains_first, gains_second, token_table, table_first, table_second, place_table, place_first, place_second):
    masters = (entry_weight, exit_weight, expand_weight, reduce_weight, norm_gains, token_table, place_table)
    firsts = (entry_first, exit_first, expand_first, reduce_first, gains_first, table_first, place_first)
    seconds = (entry_second, exit_second, expand_second, reduce_second, gains_second, table_second, place_second)
    rates = (LEARN_RATE, LEARN_RATE, LEARN_RATE, LEARN_RATE, GAIN_RATE, LEARN_RATE, LEARN_RATE)
    count = jnp.sum((score_places < target_lengths[:, None]).astype(jnp.float32))
    data = (source_ids, target_ids, score_places, target_labels, source_lengths, target_lengths)
    one_pair = jax.checkpoint(lambda used, item: pair_loss(used, item, count))

    def total_loss(params):
        entry, leave, expand, shrink, gains, table, places = params
        used = (low(entry), low(leave), low(expand), low(shrink), gains, low(table), low(places))

        def visit(carry, item):
            loss, losses = one_pair(used, item)
            return (carry + loss, losses)
        return lax.scan(visit, jnp.zeros((), jnp.float32), data)
    mean_loss, pullback, losses = jax.vjp(total_loss, masters, has_aux=True)
    grads = pullback(jnp.ones((), jnp.float32))[0]
    square = jnp.zeros((), jnp.float32)
    for grad in grads:
        square = square + jnp.sum(grad * grad)
    gradient_norm = jnp.sqrt(square)
    clip = jnp.minimum(1.0, MAX_NORM / (gradient_norm + 1e-06))
    steps = step_count[0].astype(jnp.float32)
    fix_one = 1 - FIRST_DECAY ** steps
    fix_two = 1 - SECOND_DECAY ** steps
    pair_losses = jnp.zeros_like(losses).at[pair_order].set(losses)
    results = [mean_loss, gradient_norm, pair_losses]
    for master, first, second, grad, rate in zip(masters, firsts, seconds, grads, rates):
        results.extend(adam_step(master, first, second, grad, clip, fix_one, fix_two, rate))
    return tuple(results)
```

```python
import jax
import jax.numpy as jnp
from jax import lax
from jax.sharding import PartitionSpec as P

HEAD_DIM = 64
MAX_NORM = 0.01
LEARN_RATE = 0.03
GAIN_RATE = 0.3
FIRST_DECAY = 0.9
SECOND_DECAY = 0.999
ADAM_EPSILON = 1e-08
WEIGHT_DECAY = 0.01
SCORE_FLOOR = -1000000000.0
EVERY = ("dp", "tensor")
CORE_SWAP = ((0, 1), (1, 0))
SLOTS = 32


def norm_rows(values, gain):
    centered = values - jnp.mean(values, axis=-1, keepdims=True)
    variance = jnp.mean(centered * centered, axis=-1, keepdims=True)
    return centered * lax.rsqrt(variance + 1e-05) * gain


def swap(values):
    return lax.ppermute(values, "tensor", CORE_SWAP)


def spread(rows):
    return jnp.concatenate([rows, swap(rows)], axis=0)


def collect(partial_rows):
    half = partial_rows.shape[0] // 2
    return partial_rows[:half] + swap(partial_rows[half:])


def to_all(values, axis=EVERY):
    size = lax.axis_size(axis)
    return lax.all_to_all(
        jnp.broadcast_to(values[None], (size,) + values.shape), axis, 0, 0, tiled=True
    )


def product(left, right):
    return jnp.dot(left, right, preferred_element_type=jnp.float32)


def product_tn(left, right):
    return lax.dot_general(
        left, right, (((0,), (0,)), ((), ())), preferred_element_type=jnp.float32
    )


def product_nt(left, right):
    return lax.dot_general(
        left, right, (((1,), (1,)), ((), ())), preferred_element_type=jnp.float32
    )


def heads_of(values):
    return values.reshape(values.shape[0], values.shape[1] // HEAD_DIM, HEAD_DIM)


def scores_for(query, key, allowed):
    raw = jnp.einsum(
        "qhd,khd->hqk", heads_of(query), heads_of(key), preferred_element_type=jnp.float32
    )
    return jnp.where(allowed[None], raw * HEAD_DIM ** (-0.5), SCORE_FLOOR)


def attend_forward(query, key, value, allowed):
    scores = scores_for(query, key, allowed)
    highest = jnp.max(scores, axis=-1, keepdims=True)
    log_total = highest + jnp.log(jnp.sum(jnp.exp(scores - highest), axis=-1, keepdims=True))
    weights = jnp.exp(scores - log_total).astype(jnp.bfloat16)
    mixed = jnp.einsum(
        "hqk,khd->qhd", weights, heads_of(value), preferred_element_type=jnp.float32
    )
    return mixed.astype(jnp.bfloat16).reshape(query.shape), log_total


def attend_backward(query, key, value, log_total, grad_mixed, allowed):
    grad_heads = heads_of(grad_mixed)
    weights = jnp.exp(scores_for(query, key, allowed) - log_total)
    grad_value = jnp.einsum(
        "hqk,qhd->khd",
        weights.astype(jnp.bfloat16),
        grad_heads,
        preferred_element_type=jnp.float32,
    )
    grad_weights = jnp.einsum(
        "qhd,khd->hqk", grad_heads, heads_of(value), preferred_element_type=jnp.float32
    )
    inner = jnp.sum(weights * grad_weights, axis=-1, keepdims=True)
    grad_scores = (weights * (grad_weights - inner) * HEAD_DIM ** (-0.5)).astype(jnp.bfloat16)
    grad_query = jnp.einsum(
        "hqk,khd->qhd", grad_scores, heads_of(key), preferred_element_type=jnp.float32
    )
    grad_key = jnp.einsum(
        "hqk,qhd->khd", grad_scores, heads_of(query), preferred_element_type=jnp.float32
    )
    return tuple(
        grad.astype(jnp.bfloat16).reshape(query.shape)
        for grad in (grad_query, grad_key, grad_value)
    )


def attention_forward(stream, gain, weights, allowed, memory):
    gathered = spread(norm_rows(stream, gain).astype(jnp.bfloat16))
    source = gathered if memory is None else memory
    query = product(gathered, weights[0]).astype(jnp.bfloat16)
    key = product(source, weights[1]).astype(jnp.bfloat16)
    value = product(source, weights[2]).astype(jnp.bfloat16)
    mixed, log_total = attend_forward(query, key, value, allowed)
    output = collect(product_nt(mixed, weights[3]))
    return (output, (stream, gathered, query, key, value, mixed, log_total))


def attention_backward(grad_out, gain, weights, allowed, memory, saved):
    stream, gathered, query, key, value, mixed, log_total = saved
    grad_rows = spread(grad_out.astype(jnp.bfloat16))
    grad_leave = product_tn(grad_rows, mixed)
    grad_mixed = product(grad_rows, weights[3]).astype(jnp.bfloat16)
    grad_query, grad_key, grad_value = attend_backward(
        query, key, value, log_total, grad_mixed, allowed
    )
    source = gathered if memory is None else memory
    grads = (
        product_tn(gathered, grad_query),
        product_tn(source, grad_key),
        product_tn(source, grad_value),
        grad_leave,
    )
    back_query = product_nt(grad_query, weights[0])
    back_source = product_nt(grad_key, weights[1]) + product_nt(grad_value, weights[2])
    if memory is None:
        grad_normed = collect(back_query + back_source)
        grad_memory = None
    else:
        grad_normed = collect(back_query)
        grad_memory = collect(back_source)
    grad_stream, grad_gain = jax.vjp(norm_rows, stream, gain)[1](grad_normed)
    return (grad_stream + grad_out, grad_gain, grads, grad_memory)


def gelu_exact(values):
    return jax.nn.gelu(values, approximate=False)


def feed_forward(stream, gain, weights):
    gathered = spread(norm_rows(stream, gain).astype(jnp.bfloat16))
    inner = product(gathered, weights[0])
    hidden = gelu_exact(inner).astype(jnp.bfloat16)
    output = collect(product_nt(hidden, weights[1]))
    return (output, (stream, gathered, inner, hidden))


def feed_backward(grad_out, gain, weights, saved):
    stream, gathered, inner, hidden = saved
    grad_rows = spread(grad_out.astype(jnp.bfloat16))
    grad_shrink = product_tn(grad_rows, hidden)
    grad_hidden = product(grad_rows, weights[1]).astype(jnp.bfloat16)
    grad_inner = jax.vjp(gelu_exact, inner)[1](grad_hidden.astype(jnp.float32))[0].astype(
        jnp.bfloat16
    )
    grad_expand = product_tn(gathered, grad_inner)
    grad_normed = collect(product_nt(grad_inner, weights[0]))
    grad_stream, grad_gain = jax.vjp(norm_rows, stream, gain)[1](grad_normed)
    return (grad_stream + grad_out, grad_gain, (grad_expand, grad_shrink))


def adam_step(master, first, second, grad, clip, fix_one, fix_two, rate):
    grad = grad * clip
    first_new = FIRST_DECAY * first + (1 - FIRST_DECAY) * grad
    second_new = SECOND_DECAY * second + (1 - SECOND_DECAY) * grad * grad
    master_new = master - rate * (
        first_new / fix_one / (jnp.sqrt(second_new / fix_two) + ADAM_EPSILON)
        + WEIGHT_DECAY * master
    )
    return (master_new, first_new, second_new)


def gather_weights(shards):
    return lax.all_gather(shards, "dp", axis=1, tiled=True)


def scatter_grads(grads):
    stacked = jnp.stack([grad.astype(jnp.bfloat16) for grad in grads])
    return lax.psum_scatter(stacked, "dp", scatter_dimension=1, tiled=True).astype(jnp.float32)


def flipped(values):
    return jnp.swapaxes(values, -1, -2)


def request_slots(ids, rows_owned):
    owner = ids // rows_owned
    here = jnp.arange(ids.shape[0])
    earlier = here[None, :] < here[:, None]
    same = ids[:, None] == ids[None, :]
    leads = jnp.sum((same & earlier).astype(jnp.int32), axis=1) == 0
    leader = jnp.min(jnp.where(same, here[None, :], ids.shape[0]), axis=1)
    rank = jnp.sum(
        (
            (here[None, :] < leader[:, None])
            & leads[None, :]
            & (owner[:, None] == owner[None, :])
        ).astype(jnp.int32),
        axis=1,
    )
    return owner, rank, leads


def chosen_rows(index, count, dtype=jnp.bfloat16):
    return (index[:, None] == jnp.arange(count)[None, :]).astype(dtype)


def local(
    source_ids,
    target_ids,
    score_places,
    target_labels,
    source_lengths,
    target_lengths,
    pair_order,
    step_count,
    entry_weight,
    entry_first,
    entry_second,
    exit_weight,
    exit_first,
    exit_second,
    expand_weight,
    expand_first,
    expand_second,
    reduce_weight,
    reduce_first,
    reduce_second,
    norm_gains,
    gains_first,
    gains_second,
    token_table,
    table_first,
    table_second,
    place_table,
    place_first,
    place_second,
):
    groups = lax.axis_size("dp")
    parts = lax.axis_size("tensor")
    devices = groups * parts
    group = lax.axis_index("dp")
    part = lax.axis_index("tensor")
    low = jnp.bfloat16
    rows_owned, width = token_table.shape
    half = source_ids.shape[1]
    spot_share = score_places.shape[1]

    blocks = entry_weight.shape[3]
    entry_low = entry_weight.astype(low)
    leave_low = flipped(exit_weight.astype(low))
    place_low = flipped(place_table.astype(low))
    place_low = jnp.pad(place_low, ((0, 0), (0, 0), (0, blocks - half)))
    expand_low = expand_weight.astype(low)
    shrink_low = flipped(reduce_weight.astype(low))
    narrow = gather_weights(
        jnp.concatenate(
            [
                entry_low[0],
                leave_low[:1],
                entry_low[1],
                leave_low[1:2],
                entry_low[2],
                leave_low[2:],
                place_low,
            ]
        )
    )
    attend_weights = [[narrow[4 * a + b] for b in range(4)] for a in range(3)]
    places = flipped(narrow[12:14, :, :half])
    feed_weights = [
        gather_weights(jnp.stack([expand_low[b], shrink_low[b]])) for b in range(2)
    ]

    ids = jnp.concatenate([source_ids[0], target_ids[0]])
    owner, rank, leads = request_slots(ids, rows_owned)
    rounds = jnp.max(rank) // SLOTS + 1
    slots_all = devices * SLOTS
    slot_names = jnp.arange(slots_all)

    def slot_in(turn):
        return jnp.where(rank // SLOTS == turn, owner * SLOTS + rank % SLOTS, -1)

    def requests_in(turn):
        asked = (slot_names[:, None] == slot_in(turn)[None, :]) & leads[None, :]
        return jnp.sum(
            jnp.where(asked, ids[None, :] % rows_owned + 1, 0), axis=1
        ).reshape(devices, SLOTS)

    spots = score_places[0]
    extras = jnp.concatenate(
        [
            spots,
            target_labels[0],
            (spots < target_lengths[0]).astype(jnp.int32),
            rounds[None],
        ]
    )
    message = jnp.concatenate(
        [
            requests_in(0),
            jnp.broadcast_to(extras[None], (devices, extras.shape[0])),
        ],
        axis=1,
    )
    heard = lax.all_to_all(message, EVERY, 0, 0, tiled=True)
    asked_first = heard[:, :SLOTS].reshape(-1) - 1
    spots_all = heard[:, SLOTS : SLOTS + spot_share]
    labels_all = heard[:, SLOTS + spot_share : SLOTS + 2 * spot_share]
    valid_all = heard[:, SLOTS + 2 * spot_share : SLOTS + 3 * spot_share]
    rounds_all = jnp.max(heard[:, -1])
    own_table = token_table.astype(low)

    def looked_up(asked, slot):
        sent = product(chosen_rows(asked, rows_owned), own_table).astype(low)
        got = lax.all_to_all(
            sent.reshape(devices, SLOTS, width), EVERY, 0, 0, tiled=True
        ).reshape(slots_all, width)
        return product(chosen_rows(slot, slots_all), got)

    def ask_again(turn):
        return (
            lax.all_to_all(requests_in(turn), EVERY, 0, 0, tiled=True).reshape(-1) - 1
        )

    start = looked_up(asked_first, slot_in(0))
    start = lax.while_loop(
        lambda state: state[0] < rounds_all,
        lambda state: (
            state[0] + 1,
            state[1] + looked_up(ask_again(state[0]), slot_in(state[0])),
        ),
        (jnp.int32(1), start),
    )[1]
    start = start.reshape(2, half, width) + places.astype(jnp.float32)

    row_places = jnp.concatenate(
        [part * half + jnp.arange(half), (1 - part) * half + jnp.arange(half)]
    )
    length = row_places.shape[0]
    encoder_mask = jnp.broadcast_to(row_places[None, :] < source_lengths[0], (length, length))
    decoder_mask = (row_places[None, :] <= row_places[:, None]) & (
        row_places[None, :] < target_lengths[0]
    )
    stream = start[0]
    output, enc_attend = attention_forward(
        stream, norm_gains[0], attend_weights[0], encoder_mask, None
    )
    stream = stream + output
    decoded = start[1]
    output, dec_self = attention_forward(
        decoded, norm_gains[3], attend_weights[1], decoder_mask, None
    )
    decoded = decoded + output
    output, enc_feed = feed_forward(stream, norm_gains[1], feed_weights[0])
    stream = stream + output
    memory = spread(norm_rows(stream, norm_gains[2]).astype(low))
    output, dec_cross = attention_forward(
        decoded, norm_gains[4], attend_weights[2], encoder_mask, memory
    )
    decoded = decoded + output
    output, dec_feed = feed_forward(decoded, norm_gains[5], feed_weights[1])
    decoded = decoded + output
    final = spread(norm_rows(decoded, norm_gains[6]).astype(low))

    picked_own = product(
        (spots[:, None] == row_places[None, :]).astype(low), final
    ).astype(low)
    picked_group = to_all(picked_own, "dp")
    picked = jnp.concatenate([picked_group, swap(picked_group)]).reshape(-1, width)
    scored = picked.shape[0]

    def own_first(values):
        values = values.reshape(groups, parts, spot_share)
        mine = jnp.where(part == 0, values[:, 0], values[:, 1])
        theirs = jnp.where(part == 0, values[:, 1], values[:, 0])
        return jnp.stack([mine, theirs]).reshape(-1)

    def own_second(values):
        values = values.reshape(parts, groups, spot_share)
        zero = jnp.where(part == 0, values[0], values[1])
        one = jnp.where(part == 0, values[1], values[0])
        return jnp.stack([zero, one], axis=1).reshape(-1)

    label_row = own_first(labels_all) - (group * parts + part) * rows_owned
    valid = own_first(valid_all).astype(jnp.float32)
    count = jnp.sum(valid_all.astype(jnp.float32))
    logits = product_nt(picked, own_table)
    onehot = chosen_rows(label_row, rows_owned, jnp.bool_)
    highest = jnp.max(logits, axis=-1)
    log_here = highest + jnp.log(jnp.sum(jnp.exp(logits - highest[:, None]), axis=-1))
    golden_here = jnp.sum(jnp.where(onehot, logits, 0.0), axis=-1)
    stats = to_all(jnp.stack([own_second(log_here), own_second(golden_here)]))
    top = jnp.max(stats[:, 0], axis=0)
    log_total = top + jnp.log(jnp.sum(jnp.exp(stats[:, 0] - top[None]), axis=0))
    golden = jnp.sum(stats[:, 1], axis=0)
    losses = (log_total - golden) * valid_all.reshape(-1).astype(jnp.float32)
    mean_loss = jnp.sum(losses) / count
    of_group = (pair_order == group).astype(jnp.float32)
    pair_rows = jnp.sum(
        losses.reshape(groups, parts, spot_share) * of_group[:, None, None], axis=0
    )
    pair_losses = jnp.where(part == 0, pair_rows[0], pair_rows[1])[None]
    probs = jnp.exp(logits - own_first(log_total)[:, None])
    grad_logits = (
        (probs - onehot.astype(jnp.float32)) * (valid / count)[:, None]
    ).astype(low)
    grad_picked = collect(product(grad_logits, own_table))
    grad_picked = lax.all_to_all(
        grad_picked.astype(low).reshape(groups, spot_share, width), "dp", 0, 0, tiled=True
    )
    grad_picked = spread(jnp.sum(grad_picked.astype(jnp.float32), axis=0))
    spots_group = own_first(spots_all).reshape(parts, groups, spot_share)
    spots_group = lax.dynamic_index_in_dim(spots_group, group, 1, False).reshape(-1)
    grad_final = jnp.dot(
        (row_places[:half, None] == spots_group[None, :]).astype(jnp.float32),
        grad_picked,
        precision=lax.Precision.HIGHEST,
        preferred_element_type=jnp.float32,
    )
    grad_table = product_tn(grad_logits, picked)

    grad_decoded, gain_six = jax.vjp(norm_rows, decoded, norm_gains[6])[1](grad_final)
    saved_decoded = dec_feed[0]
    grad_decoded, gain_five, feed_one = feed_backward(
        grad_decoded, norm_gains[5], feed_weights[1], dec_feed
    )
    feed_one = scatter_grads(feed_one)
    grad_decoded, gain_four, attend_two, grad_memory = attention_backward(
        grad_decoded, norm_gains[4], attend_weights[2], encoder_mask, memory, dec_cross
    )
    grad_stream, gain_two = jax.vjp(norm_rows, stream, norm_gains[2])[1](grad_memory)
    grad_stream, gain_one, feed_zero = feed_backward(
        grad_stream, norm_gains[1], feed_weights[0], enc_feed
    )
    feed_zero = scatter_grads(feed_zero)
    grad_decoded, gain_three, attend_one, unused_one = attention_backward(
        grad_decoded, norm_gains[3], attend_weights[1], decoder_mask, None, dec_self
    )
    middle = scatter_grads(attend_two + attend_one)
    grad_stream, gain_zero, attend_zero, unused_zero = attention_backward(
        grad_stream, norm_gains[0], attend_weights[0], encoder_mask, None, enc_attend
    )
    grad_start = jnp.stack([grad_stream, grad_decoded]).astype(low)
    place_grads = jnp.pad(flipped(grad_start), ((0, 0), (0, 0), (0, blocks - half)))
    last = scatter_grads(attend_zero + (place_grads[0], place_grads[1]))

    start_rows = grad_start.reshape(2 * half, width)

    def returned(asked, slot):
        sent = product_tn(chosen_rows(slot, slots_all), start_rows).astype(low)
        got = lax.all_to_all(
            sent.reshape(devices, SLOTS, width), EVERY, 0, 0, tiled=True
        ).reshape(slots_all, width)
        return product_tn(chosen_rows(asked, rows_owned), got)

    table_grad = grad_table + returned(asked_first, slot_in(0))
    table_grad = lax.while_loop(
        lambda state: state[0] < rounds_all,
        lambda state: (
            state[0] + 1,
            state[1] + returned(ask_again(state[0]), slot_in(state[0])),
        ),
        (jnp.int32(1), table_grad),
    )[1]

    gain_partial = jnp.stack(
        [gain_zero, gain_one, gain_two, gain_three, gain_four, gain_five, gain_six]
    )
    gain_own = jnp.sum(
        lax.all_to_all(gain_partial.reshape(devices, -1), EVERY, 0, 0, tiled=True), axis=0
    )
    entry_grad = jnp.stack([last[:3], middle[4:7], middle[:3]])
    leave_grad = flipped(jnp.stack([last[3], middle[7], middle[3]]))
    expand_grad = jnp.stack([feed_zero[0], feed_one[0]])
    shrink_grad = flipped(jnp.stack([feed_zero[1], feed_one[1]]))
    place_grad = flipped(last[4:6, :, :half])
    squares = jnp.sum(gain_own * gain_own)
    for grad in (entry_grad, leave_grad, expand_grad, shrink_grad, table_grad, place_grad):
        squares = squares + jnp.sum(grad * grad)
    last_words = to_all(jnp.concatenate([gain_own, squares[None]]))
    gain_grad = last_words[:, :-1].reshape(norm_gains.shape)
    gradient_norm = jnp.sqrt(jnp.sum(last_words[:, -1]))
    clip = jnp.minimum(1.0, MAX_NORM / (gradient_norm + 1e-06))
    steps = step_count[0].astype(jnp.float32)
    fix_one = 1 - FIRST_DECAY**steps
    fix_two = 1 - SECOND_DECAY**steps
    masters = (
        entry_weight,
        exit_weight,
        expand_weight,
        reduce_weight,
        norm_gains,
        token_table,
        place_table,
    )
    firsts = (
        entry_first,
        exit_first,
        expand_first,
        reduce_first,
        gains_first,
        table_first,
        place_first,
    )
    seconds = (
        entry_second,
        exit_second,
        expand_second,
        reduce_second,
        gains_second,
        table_second,
        place_second,
    )
    grads = (entry_grad, leave_grad, expand_grad, shrink_grad, gain_grad, table_grad, place_grad)
    rates = (LEARN_RATE, LEARN_RATE, LEARN_RATE, LEARN_RATE, GAIN_RATE, LEARN_RATE, LEARN_RATE)
    results = [mean_loss, gradient_norm, pair_losses]
    for master, first, second, grad, rate in zip(masters, firsts, seconds, grads, rates):
        results.extend(adam_step(master, first, second, grad, clip, fix_one, fix_two, rate))
    return tuple(results)


def solution(mesh):
    return jax.shard_map(
        local,
        mesh=mesh,
        in_specs=(
            P("dp", "tensor"),
            P("dp", "tensor"),
            P("dp", "tensor"),
            P("dp", "tensor"),
            P("dp"),
            P("dp"),
            P(),
            P(),
            P(None, None, "dp", "tensor"),
            P(None, None, "dp", "tensor"),
            P(None, None, "dp", "tensor"),
            P(None, "tensor", "dp"),
            P(None, "tensor", "dp"),
            P(None, "tensor", "dp"),
            P(None, "dp", "tensor"),
            P(None, "dp", "tensor"),
            P(None, "dp", "tensor"),
            P(None, "tensor", "dp"),
            P(None, "tensor", "dp"),
            P(None, "tensor", "dp"),
            P(),
            P(),
            P(),
            P(("dp", "tensor"), None),
            P(("dp", "tensor"), None),
            P(("dp", "tensor"), None),
            P(None, "tensor", "dp"),
            P(None, "tensor", "dp"),
            P(None, "tensor", "dp"),
        ),
        out_specs=(
            P(),
            P(),
            P("dp", "tensor"),
            P(None, None, "dp", "tensor"),
            P(None, None, "dp", "tensor"),
            P(None, None, "dp", "tensor"),
            P(None, "tensor", "dp"),
            P(None, "tensor", "dp"),
            P(None, "tensor", "dp"),
            P(None, "dp", "tensor"),
            P(None, "dp", "tensor"),
            P(None, "dp", "tensor"),
            P(None, "tensor", "dp"),
            P(None, "tensor", "dp"),
            P(None, "tensor", "dp"),
            P(),
            P(),
            P(),
            P(("dp", "tensor"), None),
            P(("dp", "tensor"), None),
            P(("dp", "tensor"), None),
            P(None, "tensor", "dp"),
            P(None, "tensor", "dp"),
            P(None, "tensor", "dp"),
        ),
        check_vma=False,
    )
```

```python
import jax
import jax.numpy as jnp
from jax import lax
from jax.sharding import PartitionSpec as P

HEAD_DIM = 64
MAX_NORM = 0.01
LEARN_RATE = 0.03
GAIN_RATE = 0.3
FIRST_DECAY = 0.9
SECOND_DECAY = 0.999
ADAM_EPSILON = 1e-08
WEIGHT_DECAY = 0.01
SCORE_FLOOR = -1000000000.0
EVERY = ("dp", "tensor")
CORE_SWAP = ((0, 1), (1, 0))
SLOTS = 32


def norm_rows(values, gain):
    centered = values - jnp.mean(values, axis=-1, keepdims=True)
    variance = jnp.mean(centered * centered, axis=-1, keepdims=True)
    return centered * lax.rsqrt(variance + 1e-05) * gain


def swap(values):
    return lax.ppermute(values, "tensor", CORE_SWAP)


def spread(rows):
    return jnp.concatenate([rows, swap(rows)], axis=0)


def collect(partial_rows):
    half = partial_rows.shape[0] // 2
    return partial_rows[:half] + swap(partial_rows[half:])


def to_all(values, axis=EVERY):
    size = lax.axis_size(axis)
    return lax.all_to_all(
        jnp.broadcast_to(values[None], (size,) + values.shape), axis, 0, 0, tiled=True
    )


def product(left, right):
    return jnp.dot(left, right, preferred_element_type=jnp.float32)


def product_tn(left, right):
    return lax.dot_general(
        left, right, (((0,), (0,)), ((), ())), preferred_element_type=jnp.float32
    )


def product_nt(left, right):
    return lax.dot_general(
        left, right, (((1,), (1,)), ((), ())), preferred_element_type=jnp.float32
    )


def heads_of(values):
    return values.reshape(values.shape[0], values.shape[1] // HEAD_DIM, HEAD_DIM)


def scores_for(query, key, allowed):
    raw = jnp.einsum(
        "qhd,khd->hqk", heads_of(query), heads_of(key), preferred_element_type=jnp.float32
    )
    return jnp.where(allowed[None], raw * HEAD_DIM ** (-0.5), SCORE_FLOOR)


def attend_forward(query, key, value, allowed):
    scores = scores_for(query, key, allowed)
    highest = jnp.max(scores, axis=-1, keepdims=True)
    log_total = highest + jnp.log(jnp.sum(jnp.exp(scores - highest), axis=-1, keepdims=True))
    weights = jnp.exp(scores - log_total).astype(jnp.bfloat16)
    mixed = jnp.einsum(
        "hqk,khd->qhd", weights, heads_of(value), preferred_element_type=jnp.float32
    )
    return mixed.astype(jnp.bfloat16).reshape(query.shape), log_total


def attend_backward(query, key, value, log_total, grad_mixed, allowed):
    grad_heads = heads_of(grad_mixed)
    weights = jnp.exp(scores_for(query, key, allowed) - log_total)
    grad_value = jnp.einsum(
        "hqk,qhd->khd",
        weights.astype(jnp.bfloat16),
        grad_heads,
        preferred_element_type=jnp.float32,
    )
    grad_weights = jnp.einsum(
        "qhd,khd->hqk", grad_heads, heads_of(value), preferred_element_type=jnp.float32
    )
    inner = jnp.sum(weights * grad_weights, axis=-1, keepdims=True)
    grad_scores = (weights * (grad_weights - inner) * HEAD_DIM ** (-0.5)).astype(jnp.bfloat16)
    grad_query = jnp.einsum(
        "hqk,khd->qhd", grad_scores, heads_of(key), preferred_element_type=jnp.float32
    )
    grad_key = jnp.einsum(
        "hqk,qhd->khd", grad_scores, heads_of(query), preferred_element_type=jnp.float32
    )
    return tuple(
        grad.astype(jnp.bfloat16).reshape(like.shape)
        for grad, like in ((grad_query, query), (grad_key, key), (grad_value, value))
    )


def pick_rows(index, rows):
    return product(index, rows).astype(jnp.bfloat16)


def place_exact(index, rows):
    return jnp.dot(
        index.astype(jnp.float32),
        rows,
        precision=lax.Precision.HIGHEST,
        preferred_element_type=jnp.float32,
    )


def both(partial_rows):
    return partial_rows + swap(partial_rows)


def norm_backward(values, gain, grad):
    grad_values, grad_gain = jax.vjp(norm_rows, values, gain)[1](grad)
    return grad_values, grad_gain


def own_half(rows):
    half = rows.shape[0] // 2
    return jnp.where(lax.axis_index("tensor") == 0, rows[:half], rows[half:])


def in_order(rows):
    other = swap(rows)
    return jnp.where(
        lax.axis_index("tensor") == 0,
        jnp.concatenate([rows, other]),
        jnp.concatenate([other, rows]),
    )


def norm_backward_shared(values, gain, grad):
    grad_values = jax.vjp(lambda rows: norm_rows(rows, gain), values)[1](grad)[0]
    own = own_half(values)
    grad_gain = jax.vjp(lambda scale: norm_rows(own, scale), gain)[1](own_half(grad))[0]
    return grad_values, grad_gain


def low_rounded(*values):
    return tuple(value.astype(jnp.bfloat16) for value in values)


def encode_attention(stream, gain, weights, allowed):
    gathered = spread(norm_rows(stream, gain).astype(jnp.bfloat16))
    query, key, value = low_rounded(*[product(gathered, weights[b]) for b in range(3)])
    mixed, log_total = attend_forward(query, key, value, allowed)
    output = collect(product_nt(mixed, weights[3]))
    return (output, (stream, gathered, query, key, value, mixed, log_total))


def encode_attention_backward(grad_out, gain, weights, allowed, saved):
    stream, gathered, query, key, value, mixed, log_total = saved
    grad_rows = spread(grad_out.astype(jnp.bfloat16))
    grad_leave = product_tn(grad_rows, mixed)
    grad_mixed = product(grad_rows, weights[3]).astype(jnp.bfloat16)
    inner_grads = attend_backward(query, key, value, log_total, grad_mixed, allowed)
    grads = [product_tn(gathered, grad) for grad in inner_grads]
    back = sum(product_nt(grad, weight) for grad, weight in zip(inner_grads, weights))
    grad_stream, grad_gain = norm_backward(stream, gain, collect(back))
    return (grad_stream + grad_out, grad_gain, low_rounded(*grads, grad_leave))


def decode_attention(rows, source, weights, allowed):
    query = product(rows, weights[0]).astype(jnp.bfloat16)
    key, value = low_rounded(product(source, weights[1]), product(source, weights[2]))
    mixed, log_total = attend_forward(query, key, value, allowed)
    output = both(product_nt(mixed, weights[3]))
    return (output, (rows, source, query, key, value, mixed, log_total))


def decode_attention_backward(grad_out, weights, allowed, saved):
    rows, source, query, key, value, mixed, log_total = saved
    grad_rows = grad_out.astype(jnp.bfloat16)
    grad_leave = product_tn(grad_rows, mixed)
    grad_mixed = product(grad_rows, weights[3]).astype(jnp.bfloat16)
    grad_query, grad_key, grad_value = attend_backward(
        query, key, value, log_total, grad_mixed, allowed
    )
    grads = low_rounded(
        product_tn(rows, grad_query),
        product_tn(source, grad_key),
        product_tn(source, grad_value),
        grad_leave,
    )
    back_rows = product_nt(grad_query, weights[0])
    back_source = product_nt(grad_key, weights[1]) + product_nt(grad_value, weights[2])
    return (back_rows, back_source, grads)


def gelu_exact(values):
    return jax.nn.gelu(values, approximate=False)


def feed_forward(stream, gain, weights):
    gathered = spread(norm_rows(stream, gain).astype(jnp.bfloat16))
    inner = product(gathered, weights[0])
    hidden = gelu_exact(inner).astype(jnp.bfloat16)
    output = collect(product_nt(hidden, weights[1]))
    return (output, (stream, gathered, inner, hidden))


def feed_backward(grad_out, gain, weights, saved):
    stream, gathered, inner, hidden = saved
    grad_rows = spread(grad_out.astype(jnp.bfloat16))
    grad_shrink = product_tn(grad_rows, hidden).astype(jnp.bfloat16)
    grad_hidden = product(grad_rows, weights[1]).astype(jnp.bfloat16)
    grad_inner = jax.vjp(gelu_exact, inner)[1](grad_hidden.astype(jnp.float32))[0].astype(
        jnp.bfloat16
    )
    grad_expand = product_tn(gathered, grad_inner).astype(jnp.bfloat16)
    grad_normed = collect(product_nt(grad_inner, weights[0]))
    grad_stream, grad_gain = jax.vjp(norm_rows, stream, gain)[1](grad_normed)
    return (grad_stream + grad_out, grad_gain, (grad_expand, grad_shrink))


def decode_feed(rows, weights):
    inner = product(rows, weights[0])
    hidden = gelu_exact(inner).astype(jnp.bfloat16)
    return (both(product_nt(hidden, weights[1])), (rows, inner, hidden))


def decode_feed_backward(grad_out, weights, saved):
    rows, inner, hidden = saved
    grad_rows = grad_out.astype(jnp.bfloat16)
    grad_shrink = product_tn(grad_rows, hidden)
    grad_hidden = product(grad_rows, weights[1]).astype(jnp.bfloat16)
    grad_inner = jax.vjp(gelu_exact, inner)[1](grad_hidden.astype(jnp.float32))[0].astype(
        jnp.bfloat16
    )
    grad_expand = product_tn(rows, grad_inner)
    return (both(product_nt(grad_inner, weights[0])), low_rounded(grad_expand, grad_shrink))


def adam_step(master, first, second, grad, clip, fix_one, fix_two, rate):
    grad = grad * clip
    first_new = FIRST_DECAY * first + (1 - FIRST_DECAY) * grad
    second_new = SECOND_DECAY * second + (1 - SECOND_DECAY) * grad * grad
    master_new = master - rate * (
        first_new / fix_one / (jnp.sqrt(second_new / fix_two) + ADAM_EPSILON)
        + WEIGHT_DECAY * master
    )
    return (master_new, first_new, second_new)


def bit_order(turn):
    count = (lax.axis_size("dp") - 1).bit_length()
    order = list(range(count - 1, -1, -1))
    if turn % 2:
        for first in range(0, count - 1, 2):
            order[first], order[first + 1] = order[first + 1], order[first]
    return order


def swap_bit(values, bit):
    pairs = [(group, group ^ (1 << bit)) for group in range(lax.axis_size("dp"))]
    return lax.ppermute(values, "dp", pairs)


def gather_weights(shard, turn):
    held = shard[None]
    bits = []
    for bit in bit_order(turn):
        got = swap_bit(held, bit)
        above = sum(1 for other in bits if other > bit)
        shape = (2**above, 2 ** (len(bits) - above)) + shard.shape
        held = jnp.stack([held.reshape(shape), got.reshape(shape)], axis=1)
        held = held.reshape((-1,) + shard.shape)
        bits.append(bit)
    return held.reshape(-1, shard.shape[1])


def scatter_grads(grads, turn):
    groups = lax.axis_size("dp")
    held = grads.reshape((groups, grads.shape[0] // groups, grads.shape[1]))
    bits = sorted(bit_order(turn), reverse=True)
    for bit in reversed(bit_order(turn)):
        above = bits.index(bit)
        halves = held.reshape((2**above, 2, -1) + held.shape[1:])
        got = swap_bit(halves[:, 1].astype(jnp.bfloat16), bit)
        held = halves[:, 0].astype(jnp.float32) + got.astype(jnp.float32)
        held = held.reshape((-1,) + held.shape[2:])
        bits.remove(bit)
    return held[0]


def flipped(values):
    return jnp.swapaxes(values, -1, -2)


def request_slots(ids, rows_owned):
    owner = ids // rows_owned
    here = jnp.arange(ids.shape[0])
    earlier = here[None, :] < here[:, None]
    same = ids[:, None] == ids[None, :]
    leads = jnp.sum((same & earlier).astype(jnp.int32), axis=1) == 0
    leader = jnp.min(jnp.where(same, here[None, :], ids.shape[0]), axis=1)
    rank = jnp.sum(
        (
            (here[None, :] < leader[:, None])
            & leads[None, :]
            & (owner[:, None] == owner[None, :])
        ).astype(jnp.int32),
        axis=1,
    )
    return owner, rank, leads


def chosen_rows(index, count, dtype=jnp.bfloat16):
    return (index[:, None] == jnp.arange(count)[None, :]).astype(dtype)


def local(
    source_ids,
    target_ids,
    score_places,
    target_labels,
    source_lengths,
    target_lengths,
    pair_order,
    step_count,
    entry_weight,
    entry_first,
    entry_second,
    exit_weight,
    exit_first,
    exit_second,
    expand_weight,
    expand_first,
    expand_second,
    reduce_weight,
    reduce_first,
    reduce_second,
    norm_gains,
    gains_first,
    gains_second,
    token_table,
    table_first,
    table_second,
    place_table,
    place_first,
    place_second,
):
    groups = lax.axis_size("dp")
    parts = lax.axis_size("tensor")
    devices = groups * parts
    group = lax.axis_index("dp")
    part = lax.axis_index("tensor")
    low = jnp.bfloat16
    rows_owned, width = token_table.shape
    half = source_ids.shape[1]
    spot_share = score_places.shape[1]

    share = width // groups
    feature = jnp.arange(width)
    home = (feature // share ^ group) * share + feature % share
    order = home[:, None] == feature[None, :]

    def reordered(values):
        return product(values, order.astype(low))

    def reordered_exact(values):
        return jnp.dot(
            values,
            order.astype(jnp.float32),
            precision=lax.Precision.HIGHEST,
            preferred_element_type=jnp.float32,
        )

    gains = reordered_exact(norm_gains)
    blocks = entry_weight.shape[3]
    entry_low = entry_weight.astype(low)
    leave_low = flipped(exit_weight.astype(low))
    place_low = flipped(place_table.astype(low))
    expand_low = expand_weight.astype(low)
    shrink_low = flipped(reduce_weight.astype(low))
    wide = expand_low.shape[2]

    def beside(*pieces):
        return jnp.concatenate(pieces, axis=1)

    first_two = [
        gather_weights(
            beside(entry_low[a, 0], entry_low[a, 1], entry_low[a, 2], leave_low[a], place_low[a]), a
        )
        for a in range(2)
    ]
    next_one = gather_weights(beside(expand_low[0], entry_low[2, 0], entry_low[2, 1]), 0)
    next_two = gather_weights(beside(shrink_low[0], entry_low[2, 2], leave_low[2]), 1)
    last_two = [gather_weights(expand_low[1], 0), gather_weights(shrink_low[1], 1)]

    def pieces_of(values, first, count):
        return [
            values[:, first + b * blocks : first + (b + 1) * blocks] for b in range(count)
        ]

    attend_weights = [
        pieces_of(first_two[0], 0, 4),
        pieces_of(first_two[1], 0, 4),
        pieces_of(next_one, wide, 2) + pieces_of(next_two, wide, 2),
    ]
    feed_weights = [(next_one[:, :wide], next_two[:, :wide]), last_two]
    places = jnp.stack([flipped(values[:, 4 * blocks :]) for values in first_two])

    ids = jnp.concatenate([source_ids[0], target_ids[0]])
    owner, rank, leads = request_slots(ids, rows_owned)
    rounds = jnp.max(rank) // SLOTS + 1
    slots_all = devices * SLOTS
    slot_names = jnp.arange(slots_all)

    def slot_in(turn):
        return jnp.where(rank // SLOTS == turn, owner * SLOTS + rank % SLOTS, -1)

    def requests_in(turn):
        asked = (slot_names[:, None] == slot_in(turn)[None, :]) & leads[None, :]
        return jnp.sum(
            jnp.where(asked, ids[None, :] % rows_owned + 1, 0), axis=1
        ).reshape(devices, SLOTS)

    spots = score_places[0]
    extras = jnp.concatenate(
        [
            spots,
            target_labels[0],
            (spots < target_lengths[0]).astype(jnp.int32),
            rounds[None],
        ]
    )
    message = jnp.concatenate(
        [
            requests_in(0),
            jnp.broadcast_to(extras[None], (devices, extras.shape[0])),
        ],
        axis=1,
    )
    heard = lax.all_to_all(message, EVERY, 0, 0, tiled=True)
    asked_first = heard[:, :SLOTS].reshape(-1) - 1
    spots_all = heard[:, SLOTS : SLOTS + spot_share]
    labels_all = heard[:, SLOTS + spot_share : SLOTS + 2 * spot_share]
    valid_all = heard[:, SLOTS + 2 * spot_share : SLOTS + 3 * spot_share]
    rounds_all = jnp.max(heard[:, -1])
    own_table = token_table.astype(low)

    def looked_up(asked, slot):
        sent = product(chosen_rows(asked, rows_owned), own_table).astype(low)
        got = lax.all_to_all(
            sent.reshape(devices, SLOTS, width), EVERY, 0, 0, tiled=True
        ).reshape(slots_all, width)
        return product(chosen_rows(slot, slots_all), got)

    def ask_again(turn):
        return (
            lax.all_to_all(requests_in(turn), EVERY, 0, 0, tiled=True).reshape(-1) - 1
        )

    start = looked_up(asked_first, slot_in(0))
    start = lax.while_loop(
        lambda state: state[0] < rounds_all,
        lambda state: (
            state[0] + 1,
            state[1] + looked_up(ask_again(state[0]), slot_in(state[0])),
        ),
        (jnp.int32(1), start),
    )[1]
    start = reordered(start.astype(low)).reshape(2, half, width) + places.astype(jnp.float32)

    row_places = jnp.concatenate(
        [part * half + jnp.arange(half), (1 - part) * half + jnp.arange(half)]
    )
    length = row_places.shape[0]
    spots_group = lax.dynamic_index_in_dim(
        spots_all.reshape(groups, parts, spot_share), group, 0, False
    )
    spots_group = spots_group.reshape(-1)
    encoder_mask = jnp.broadcast_to(row_places[None, :] < source_lengths[0], (length, length))
    cross_mask = encoder_mask[: spots_group.shape[0]]
    decoder_mask = (row_places[None, :] <= spots_group[:, None]) & (
        row_places[None, :] < target_lengths[0]
    )
    scored_row = spots_group[:, None] == row_places[None, :]
    stream = start[0]
    output, enc_attend = encode_attention(stream, gains[0], attend_weights[0], encoder_mask)
    stream = stream + output
    target_rows = spread(start[1])
    target_normed = norm_rows(target_rows, gains[3]).astype(low)
    decoded = place_exact(scored_row, target_rows)
    output, dec_self = decode_attention(
        pick_rows(scored_row.astype(low), target_normed),
        target_normed,
        attend_weights[1],
        decoder_mask,
    )
    decoded = decoded + output
    output, enc_feed = feed_forward(stream, gains[1], feed_weights[0])
    stream = stream + output
    memory = spread(norm_rows(stream, gains[2]).astype(low))
    after_self = decoded
    output, dec_cross = decode_attention(
        norm_rows(after_self, gains[4]).astype(low), memory, attend_weights[2], cross_mask
    )
    after_cross = after_self + output
    output, dec_feed = decode_feed(norm_rows(after_cross, gains[5]).astype(low), feed_weights[1])
    after_feed = after_cross + output
    final = norm_rows(after_feed, gains[6]).astype(low)

    picked_own = reordered(own_half(final)).astype(low)
    picked_group = to_all(picked_own, "dp")
    picked = jnp.concatenate([picked_group, swap(picked_group)]).reshape(-1, width)

    def own_first(values):
        values = values.reshape(groups, parts, spot_share)
        mine = jnp.where(part == 0, values[:, 0], values[:, 1])
        theirs = jnp.where(part == 0, values[:, 1], values[:, 0])
        return jnp.stack([mine, theirs]).reshape(-1)

    def own_second(values):
        values = values.reshape(parts, groups, spot_share)
        zero = jnp.where(part == 0, values[0], values[1])
        one = jnp.where(part == 0, values[1], values[0])
        return jnp.stack([zero, one], axis=1).reshape(-1)

    label_row = own_first(labels_all) - (group * parts + part) * rows_owned
    valid = own_first(valid_all).astype(jnp.float32)
    count = jnp.sum(valid_all.astype(jnp.float32))
    logits = product_nt(picked, own_table)
    onehot = chosen_rows(label_row, rows_owned, jnp.bool_)
    highest = jnp.max(logits, axis=-1)
    log_here = highest + jnp.log(jnp.sum(jnp.exp(logits - highest[:, None]), axis=-1))
    golden_here = jnp.sum(jnp.where(onehot, logits, 0.0), axis=-1)
    stats = to_all(jnp.stack([own_second(log_here), own_second(golden_here)]))
    top = jnp.max(stats[:, 0], axis=0)
    log_total = top + jnp.log(jnp.sum(jnp.exp(stats[:, 0] - top[None]), axis=0))
    golden = jnp.sum(stats[:, 1], axis=0)
    losses = (log_total - golden) * valid_all.reshape(-1).astype(jnp.float32)
    mean_loss = jnp.sum(losses) / count
    of_group = (pair_order == group).astype(jnp.float32)
    pair_rows = jnp.sum(
        losses.reshape(groups, parts, spot_share) * of_group[:, None, None], axis=0
    )
    pair_losses = jnp.where(part == 0, pair_rows[0], pair_rows[1])[None]
    probs = jnp.exp(logits - own_first(log_total)[:, None])
    grad_logits = (
        (probs - onehot.astype(jnp.float32)) * (valid / count)[:, None]
    ).astype(low)
    grad_picked = collect(product(grad_logits, own_table))
    grad_picked = lax.all_to_all(
        grad_picked.astype(low).reshape(groups, spot_share, width), "dp", 0, 0, tiled=True
    )
    grad_picked = reordered(grad_picked.reshape(-1, width)).reshape(groups, spot_share, width)
    grad_picked = in_order(jnp.sum(grad_picked, axis=0))
    grad_table = product_tn(grad_logits, picked)

    grad_normed = grad_picked
    grad_rows, gain_six = norm_backward_shared(after_feed, gains[6], grad_normed)
    grad_normed, feed_one = decode_feed_backward(grad_rows, feed_weights[1], dec_feed)
    feed_one = [scatter_grads(feed_one[b], b) for b in range(2)]
    grad_values, gain_five = norm_backward_shared(after_cross, gains[5], grad_normed)
    grad_rows = grad_rows + grad_values
    back_rows, back_source, attend_two = decode_attention_backward(
        grad_rows, attend_weights[2], cross_mask, dec_cross
    )
    cross_grads = [scatter_grads(beside(*attend_two[2 * b : 2 * b + 2]), b) for b in range(2)]
    grad_stream, gain_two = norm_backward(stream, gains[2], collect(back_source))
    grad_stream, gain_one, feed_zero = feed_backward(
        grad_stream, gains[1], feed_weights[0], enc_feed
    )
    feed_zero = [scatter_grads(feed_zero[b], b) for b in range(2)]
    grad_values, gain_four = norm_backward_shared(after_self, gains[4], both(back_rows))
    grad_rows = grad_rows + grad_values
    back_rows, back_source, attend_one = decode_attention_backward(
        grad_rows, attend_weights[1], decoder_mask, dec_self
    )
    back_source = back_source + place_exact(scored_row.T, back_rows)
    grad_decoded, gain_three = norm_backward(start[1], gains[3], collect(back_source))
    grad_decoded = grad_decoded + place_exact(scored_row[:, :half].T, grad_rows)
    start_decoded = grad_decoded.astype(low)
    self_grads = scatter_grads(beside(*attend_one, flipped(start_decoded)), 0)
    grad_stream, gain_zero, attend_zero = encode_attention_backward(
        grad_stream, gains[0], attend_weights[0], encoder_mask, enc_attend
    )
    start_stream = grad_stream.astype(low)
    first_grads = scatter_grads(beside(*attend_zero, flipped(start_stream)), 1)

    start_rows = reordered(jnp.concatenate([start_stream, start_decoded])).astype(low)

    def returned(asked, slot):
        sent = product_tn(chosen_rows(slot, slots_all), start_rows).astype(low)
        got = lax.all_to_all(
            sent.reshape(devices, SLOTS, width), EVERY, 0, 0, tiled=True
        ).reshape(slots_all, width)
        return product_tn(chosen_rows(asked, rows_owned), got)

    table_grad = grad_table + returned(asked_first, slot_in(0))
    table_grad = lax.while_loop(
        lambda state: state[0] < rounds_all,
        lambda state: (
            state[0] + 1,
            state[1] + returned(ask_again(state[0]), slot_in(state[0])),
        ),
        (jnp.int32(1), table_grad),
    )[1]

    gain_partial = jnp.stack(
        [gain_zero, gain_one, gain_two, gain_three, gain_four, gain_five, gain_six]
    )
    gain_partial = reordered_exact(gain_partial)
    gain_own = jnp.sum(
        lax.all_to_all(gain_partial.reshape(devices, -1), EVERY, 0, 0, tiled=True), axis=0
    )
    first_pieces = pieces_of(first_grads, 0, 4)
    self_pieces = pieces_of(self_grads, 0, 4)
    cross_pieces = pieces_of(cross_grads[0], 0, 2) + pieces_of(cross_grads[1], 0, 2)
    entry_grad = jnp.stack(
        [jnp.stack(pieces[:3]) for pieces in (first_pieces, self_pieces, cross_pieces)]
    )
    leave_grad = flipped(jnp.stack([first_pieces[3], self_pieces[3], cross_pieces[3]]))
    expand_grad = jnp.stack([feed_zero[0], feed_one[0]])
    shrink_grad = flipped(jnp.stack([feed_zero[1], feed_one[1]]))
    place_grad = flipped(
        jnp.stack([first_grads[:, 4 * blocks :], self_grads[:, 4 * blocks :]])
    )
    squares = jnp.sum(gain_own * gain_own)
    for grad in (entry_grad, leave_grad, expand_grad, shrink_grad, table_grad, place_grad):
        squares = squares + jnp.sum(grad * grad)
    last_words = to_all(jnp.concatenate([gain_own, squares[None]]))
    gain_grad = last_words[:, :-1].reshape(norm_gains.shape)
    gradient_norm = jnp.sqrt(jnp.sum(last_words[:, -1]))
    clip = jnp.minimum(1.0, MAX_NORM / (gradient_norm + 1e-06))
    steps = step_count[0].astype(jnp.float32)
    fix_one = 1 - FIRST_DECAY**steps
    fix_two = 1 - SECOND_DECAY**steps
    masters = (
        entry_weight,
        exit_weight,
        expand_weight,
        reduce_weight,
        norm_gains,
        token_table,
        place_table,
    )
    firsts = (
        entry_first,
        exit_first,
        expand_first,
        reduce_first,
        gains_first,
        table_first,
        place_first,
    )
    seconds = (
        entry_second,
        exit_second,
        expand_second,
        reduce_second,
        gains_second,
        table_second,
        place_second,
    )
    grads = (entry_grad, leave_grad, expand_grad, shrink_grad, gain_grad, table_grad, place_grad)
    rates = (LEARN_RATE, LEARN_RATE, LEARN_RATE, LEARN_RATE, GAIN_RATE, LEARN_RATE, LEARN_RATE)
    results = [mean_loss, gradient_norm, pair_losses]
    for master, first, second, grad, rate in zip(masters, firsts, seconds, grads, rates):
        results.extend(adam_step(master, first, second, grad, clip, fix_one, fix_two, rate))
    return tuple(results)


def solution(mesh):
    return jax.shard_map(
        local,
        mesh=mesh,
        in_specs=(
            P("dp", "tensor"),
            P("dp", "tensor"),
            P("dp", "tensor"),
            P("dp", "tensor"),
            P("dp"),
            P("dp"),
            P(),
            P(),
            P(None, None, "dp", "tensor"),
            P(None, None, "dp", "tensor"),
            P(None, None, "dp", "tensor"),
            P(None, "tensor", "dp"),
            P(None, "tensor", "dp"),
            P(None, "tensor", "dp"),
            P(None, "dp", "tensor"),
            P(None, "dp", "tensor"),
            P(None, "dp", "tensor"),
            P(None, "tensor", "dp"),
            P(None, "tensor", "dp"),
            P(None, "tensor", "dp"),
            P(),
            P(),
            P(),
            P(("dp", "tensor"), None),
            P(("dp", "tensor"), None),
            P(("dp", "tensor"), None),
            P(None, "tensor", "dp"),
            P(None, "tensor", "dp"),
            P(None, "tensor", "dp"),
        ),
        out_specs=(
            P(),
            P(),
            P("dp", "tensor"),
            P(None, None, "dp", "tensor"),
            P(None, None, "dp", "tensor"),
            P(None, None, "dp", "tensor"),
            P(None, "tensor", "dp"),
            P(None, "tensor", "dp"),
            P(None, "tensor", "dp"),
            P(None, "dp", "tensor"),
            P(None, "dp", "tensor"),
            P(None, "dp", "tensor"),
            P(None, "tensor", "dp"),
            P(None, "tensor", "dp"),
            P(None, "tensor", "dp"),
            P(),
            P(),
            P(),
            P(("dp", "tensor"), None),
            P(("dp", "tensor"), None),
            P(("dp", "tensor"), None),
            P(None, "tensor", "dp"),
            P(None, "tensor", "dp"),
            P(None, "tensor", "dp"),
        ),
        check_vma=False,
    )
```

```python
import functools

import jax
import jax.numpy as jnp
from jax import lax
from jax.experimental import pallas as pl
from jax.experimental.pallas import tpu as pltpu
from jax.sharding import PartitionSpec as P

HEAD_DIM = 64
MAX_NORM = 0.01
LEARN_RATE = 0.03
GAIN_RATE = 0.3
FIRST_DECAY = 0.9
SECOND_DECAY = 0.999
ADAM_EPSILON = 1e-08
WEIGHT_DECAY = 0.01
SCORE_FLOOR = -1000000000.0
EVERY = ("dp", "tensor")
CORE_SWAP = ((0, 1), (1, 0))
SLOTS = 32


def norm_rows(values, gain):
    centered = values - jnp.mean(values, axis=-1, keepdims=True)
    variance = jnp.mean(centered * centered, axis=-1, keepdims=True)
    return centered * lax.rsqrt(variance + 1e-05) * gain


def swap(values):
    return lax.ppermute(values, "tensor", CORE_SWAP)


def spread(rows):
    return jnp.concatenate([rows, swap(rows)], axis=0)


def collect(partial_rows):
    half = partial_rows.shape[0] // 2
    return partial_rows[:half] + swap(partial_rows[half:])


def to_all(values, axis=EVERY):
    size = lax.axis_size(axis)
    return lax.all_to_all(
        jnp.broadcast_to(values[None], (size,) + values.shape), axis, 0, 0, tiled=True
    )


def product(left, right):
    return jnp.dot(left, right, preferred_element_type=jnp.float32)


def product_tn(left, right):
    return lax.dot_general(
        left, right, (((0,), (0,)), ((), ())), preferred_element_type=jnp.float32
    )


def product_nt(left, right):
    return lax.dot_general(
        left, right, (((1,), (1,)), ((), ())), preferred_element_type=jnp.float32
    )


def attend_forward_kernel(places, width, *refs):
    allowed_ref, mixed_ref = refs[-2:]
    allowed = allowed_ref[...] > 0
    for first in range(0, width, HEAD_DIM):
        query, key, value = [
            refs[ref][:, start + first : start + first + HEAD_DIM] for ref, start in places
        ]
        scores = jnp.where(allowed, product_nt(query, key) * HEAD_DIM ** (-0.5), SCORE_FLOOR)
        powers = jnp.exp(scores - jnp.max(scores, axis=1, keepdims=True))
        weights = powers * (1.0 / jnp.sum(powers, axis=1, keepdims=True))
        mixed = product(weights.astype(jnp.bfloat16), value)
        mixed_ref[:, first : first + HEAD_DIM] = mixed.astype(jnp.bfloat16)


def attend_backward_kernel(places, width, *refs):
    count = (len(refs) - 2) // 2
    grad_ref, allowed_ref = refs[count : count + 2]
    out_refs = refs[count + 2 :]
    allowed = allowed_ref[...] > 0
    for first in range(0, width, HEAD_DIM):
        query, key, value = [
            refs[ref][:, start + first : start + first + HEAD_DIM] for ref, start in places
        ]
        grad = grad_ref[:, first : first + HEAD_DIM]
        scores = jnp.where(allowed, product_nt(key, query) * HEAD_DIM ** (-0.5), SCORE_FLOOR)
        powers = jnp.exp(scores - jnp.max(scores, axis=0, keepdims=True))
        weights = powers * (1.0 / jnp.sum(powers, axis=0, keepdims=True))
        grad_value = product(weights.astype(jnp.bfloat16), grad)
        grad_weights = product_nt(value, grad)
        inner = jnp.sum(weights * grad_weights, axis=0, keepdims=True)
        grad_scores = (weights * (grad_weights - inner) * HEAD_DIM ** (-0.5)).astype(jnp.bfloat16)
        grads = (product_tn(grad_scores, key), product(grad_scores, query), grad_value)
        for (ref, start), values in zip(places, grads):
            out_refs[ref][:, start + first : start + first + HEAD_DIM] = values.astype(jnp.bfloat16)


def kernel_call(kernel, outputs, operands, flops):
    size = sum(value.size * value.dtype.itemsize for value in operands)
    return pl.pallas_call(
        kernel,
        out_shape=outputs,
        in_specs=[pl.BlockSpec(memory_space=pltpu.VMEM)] * len(operands),
        out_specs=jax.tree.map(lambda _: pl.BlockSpec(memory_space=pltpu.VMEM), outputs),
        compiler_params=pltpu.CompilerParams(vmem_limit_bytes=32 * 1024 * 1024),
        cost_estimate=pl.CostEstimate(flops=flops, bytes_accessed=2 * size, transcendentals=0),
    )(*operands)


def attend_forward(arrays, places, width, allowed):
    rows = arrays[places[0][0]].shape[0]
    return kernel_call(
        functools.partial(attend_forward_kernel, places, width),
        jax.ShapeDtypeStruct((rows, width), jnp.bfloat16),
        arrays + (allowed.astype(jnp.float32),),
        16 * rows * width * arrays[places[1][0]].shape[0],
    )


def attend_backward(arrays, places, width, grad_mixed, allowed):
    rows = grad_mixed.shape[0]
    return kernel_call(
        functools.partial(attend_backward_kernel, places, width),
        tuple(jax.ShapeDtypeStruct(array.shape, array.dtype) for array in arrays),
        arrays + (grad_mixed, allowed.astype(jnp.float32).T),
        40 * rows * width * arrays[places[1][0]].shape[0],
    )


def pick_rows(index, rows):
    return product(index, rows).astype(jnp.bfloat16)


def place_exact(index, rows):
    return jnp.dot(
        index.astype(jnp.float32),
        rows,
        precision=lax.Precision.HIGHEST,
        preferred_element_type=jnp.float32,
    )


def both(partial_rows):
    return partial_rows + swap(partial_rows)


def norm_backward(values, gain, grad):
    grad_values, grad_gain = jax.vjp(norm_rows, values, gain)[1](grad)
    return grad_values, grad_gain


def own_half(rows):
    half = rows.shape[0] // 2
    return jnp.where(lax.axis_index("tensor") == 0, rows[:half], rows[half:])


def in_order(rows):
    other = swap(rows)
    return jnp.where(
        lax.axis_index("tensor") == 0,
        jnp.concatenate([rows, other]),
        jnp.concatenate([other, rows]),
    )


def norm_backward_shared(values, gain, grad):
    grad_values = jax.vjp(lambda rows: norm_rows(rows, gain), values)[1](grad)[0]
    own = own_half(values)
    grad_gain = jax.vjp(lambda scale: norm_rows(own, scale), gain)[1](own_half(grad))[0]
    return grad_values, grad_gain


def tie(*values):
    return lax.optimization_barrier(values)


def low_grad(left, right):
    return product_tn(left, right).astype(jnp.bfloat16)


def low_product(left, right):
    return product(left, right).astype(jnp.bfloat16)


def gelu_exact(values):
    return jax.nn.gelu(values, approximate=False)


def gelu_backward(inner, grad_hidden):
    return jax.vjp(gelu_exact, inner)[1](grad_hidden.astype(jnp.float32))[0].astype(jnp.bfloat16)


def adam_step(master, first, second, grad, clip, fix_one, fix_two, rate):
    grad = grad * clip
    first_new = FIRST_DECAY * first + (1 - FIRST_DECAY) * grad
    second_new = SECOND_DECAY * second + (1 - SECOND_DECAY) * grad * grad
    master_new = master - rate * (
        first_new / fix_one / (jnp.sqrt(second_new / fix_two) + ADAM_EPSILON)
        + WEIGHT_DECAY * master
    )
    return (master_new, first_new, second_new)


def bit_order(turn):
    count = (lax.axis_size("dp") - 1).bit_length()
    order = list(range(count - 1, -1, -1))
    if turn % 2:
        for first in range(0, count - 1, 2):
            order[first], order[first + 1] = order[first + 1], order[first]
    return order


def swap_bit(values, bit):
    pairs = [(group, group ^ (1 << bit)) for group in range(lax.axis_size("dp"))]
    return lax.ppermute(values, "dp", pairs)


class Gather:
    def __init__(self, shard, turn):
        self.held = shard[None]
        self.order = bit_order(turn)
        self.bits = []

    def step(self):
        bit = self.order[len(self.bits)]
        got = swap_bit(self.held, bit)
        block = self.held.shape[1:]
        above = sum(1 for other in self.bits if other > bit)
        shape = (2**above, 2 ** (len(self.bits) - above)) + block
        held = jnp.stack([self.held.reshape(shape), got.reshape(shape)], axis=1)
        self.held = held.reshape((-1,) + block)
        self.bits.append(bit)

    def columns(self, first, last):
        part = Gather(self.held[0, :, first:last], 0)
        part.held, part.order, part.bits = self.held[:, :, first:last], self.order, list(self.bits)
        return part

    def left(self):
        return len(self.order) - len(self.bits)

    def rows(self):
        while self.left():
            self.step()
        return self.held.reshape(-1, self.held.shape[2])


class Scatter:
    def __init__(self, grads, turn):
        groups = lax.axis_size("dp")
        self.held = grads.reshape((groups, grads.shape[0] // groups, grads.shape[1]))
        self.order = bit_order(turn)
        self.bits = sorted(self.order, reverse=True)

    def step(self):
        bit = self.order.pop()
        above = self.bits.index(bit)
        block = self.held.shape[1:]
        halves = self.held.reshape((2**above, 2, -1) + block)
        got = swap_bit(halves[:, 1].astype(jnp.bfloat16), bit)
        held = halves[:, 0].astype(jnp.float32) + got.astype(jnp.float32)
        self.held = held.reshape((-1,) + block)
        self.bits.remove(bit)

    def left(self):
        return len(self.order)

    def rows(self):
        while self.left():
            self.step()
        return self.held[0]


def joined(scatters):
    whole = Scatter(jnp.zeros((lax.axis_size("dp"), 1)), 0)
    whole.held = jnp.concatenate([scatter.held for scatter in scatters], axis=2)
    whole.order, whole.bits = list(scatters[0].order), list(scatters[0].bits)
    return whole


def advance(movers):
    for mover in movers:
        if mover.left():
            mover.step()


def meet(value, movers):
    tied = tie(value, *[mover.held for mover in movers])
    for mover, held in zip(movers, tied[1:]):
        mover.held = held
    return tied[0]


def flipped(values):
    return jnp.swapaxes(values, -1, -2)


def request_slots(ids, rows_owned):
    owner = ids // rows_owned
    here = jnp.arange(ids.shape[0])
    earlier = here[None, :] < here[:, None]
    same = ids[:, None] == ids[None, :]
    leads = jnp.sum((same & earlier).astype(jnp.int32), axis=1) == 0
    leader = jnp.min(jnp.where(same, here[None, :], ids.shape[0]), axis=1)
    rank = jnp.sum(
        (
            (here[None, :] < leader[:, None])
            & leads[None, :]
            & (owner[:, None] == owner[None, :])
        ).astype(jnp.int32),
        axis=1,
    )
    return owner, rank, leads


def chosen_rows(index, count, dtype=jnp.bfloat16):
    return (index[:, None] == jnp.arange(count)[None, :]).astype(dtype)


def local(
    source_ids,
    target_ids,
    score_places,
    target_labels,
    source_lengths,
    target_lengths,
    pair_order,
    step_count,
    entry_weight,
    entry_first,
    entry_second,
    exit_weight,
    exit_first,
    exit_second,
    expand_weight,
    expand_first,
    expand_second,
    reduce_weight,
    reduce_first,
    reduce_second,
    norm_gains,
    gains_first,
    gains_second,
    token_table,
    table_first,
    table_second,
    place_table,
    place_first,
    place_second,
):
    groups = lax.axis_size("dp")
    parts = lax.axis_size("tensor")
    devices = groups * parts
    group = lax.axis_index("dp")
    part = lax.axis_index("tensor")
    low = jnp.bfloat16
    rows_owned, width = token_table.shape
    half = source_ids.shape[1]
    spot_share = score_places.shape[1]

    share = width // groups
    feature = jnp.arange(width)
    home = (feature // share ^ group) * share + feature % share
    order = home[:, None] == feature[None, :]

    def reordered(values):
        return product(values, order.astype(low))

    def reordered_exact(values):
        return jnp.dot(
            values,
            order.astype(jnp.float32),
            precision=lax.Precision.HIGHEST,
            preferred_element_type=jnp.float32,
        )

    gains = reordered_exact(norm_gains)
    blocks = entry_weight.shape[3]
    entry_low = entry_weight.astype(low)
    leave_low = flipped(exit_weight.astype(low))
    place_low = flipped(place_table.astype(low))
    expand_low = expand_weight.astype(low)
    shrink_low = flipped(reduce_weight.astype(low))
    wide = expand_low.shape[2]

    def beside(*pieces):
        return jnp.concatenate(pieces, axis=1)

    attend_gathers = [
        Gather(beside(entry_low[0, 0], entry_low[0, 1]), 0),
        Gather(beside(entry_low[0, 2], leave_low[0], place_low[0]), 1),
    ]
    late_gathers = [
        Gather(
            beside(entry_low[1, 0], entry_low[1, 1], entry_low[1, 2], leave_low[1], place_low[1]),
            0,
        ),
        Gather(beside(entry_low[2, 0], entry_low[2, 1], entry_low[2, 2], leave_low[2]), 1),
    ]
    advance(attend_gathers)
    feed_weights = [
        lax.all_gather(jnp.stack([expand_low[b], shrink_low[b]]), "dp", axis=1, tiled=True)
        for b in range(2)
    ]

    def pieces_of(values, first, count):
        return [
            values[:, first + b * blocks : first + (b + 1) * blocks] for b in range(count)
        ]

    ids = jnp.concatenate([source_ids[0], target_ids[0]])
    owner, rank, leads = request_slots(ids, rows_owned)
    rounds = jnp.max(rank) // SLOTS + 1
    slots_all = devices * SLOTS
    slot_names = jnp.arange(slots_all)

    def slot_in(turn):
        return jnp.where(rank // SLOTS == turn, owner * SLOTS + rank % SLOTS, -1)

    def requests_in(turn):
        asked = (slot_names[:, None] == slot_in(turn)[None, :]) & leads[None, :]
        return jnp.sum(
            jnp.where(asked, ids[None, :] % rows_owned + 1, 0), axis=1
        ).reshape(devices, SLOTS)

    spots = score_places[0]
    extras = jnp.concatenate(
        [
            spots,
            target_labels[0],
            (spots < target_lengths[0]).astype(jnp.int32),
            rounds[None],
        ]
    )
    message = jnp.concatenate(
        [
            requests_in(0),
            jnp.broadcast_to(extras[None], (devices, extras.shape[0])),
        ],
        axis=1,
    )
    heard = lax.all_to_all(message, EVERY, 0, 0, tiled=True)
    heard = meet(heard, attend_gathers)
    advance(attend_gathers)
    asked_first = heard[:, :SLOTS].reshape(-1) - 1
    spots_all = heard[:, SLOTS : SLOTS + spot_share]
    labels_all = heard[:, SLOTS + spot_share : SLOTS + 2 * spot_share]
    valid_all = heard[:, SLOTS + 2 * spot_share : SLOTS + 3 * spot_share]
    rounds_all = jnp.max(heard[:, -1])
    own_table = token_table.astype(low)

    def picked_rows(asked):
        return product(chosen_rows(asked, rows_owned), own_table).astype(low)

    def answer(sent):
        return lax.all_to_all(
            sent.reshape(devices, SLOTS, width), EVERY, 0, 0, tiled=True
        ).reshape(slots_all, width)

    def looked_up(got, slot):
        return product(chosen_rows(slot, slots_all), got)

    def ask_again(turn):
        return (
            lax.all_to_all(requests_in(turn), EVERY, 0, 0, tiled=True).reshape(-1) - 1
        )

    asked_rows = meet(picked_rows(asked_first), attend_gathers)
    got = answer(asked_rows)
    advance(attend_gathers)
    advance(attend_gathers)
    got = meet(got, attend_gathers)
    got, feed_weights[0], late_gathers[0].held, late_gathers[1].held = tie(
        got, feed_weights[0], late_gathers[0].held, late_gathers[1].held
    )
    advance(late_gathers)
    expand_zero = pick_rows(order.astype(low), feed_weights[0][0])
    shrink_zero = pick_rows(order.astype(low), feed_weights[0][1])
    start = looked_up(got, slot_in(0))
    start = lax.while_loop(
        lambda state: state[0] < rounds_all,
        lambda state: (
            state[0] + 1,
            state[1] + looked_up(answer(picked_rows(ask_again(state[0]))), slot_in(state[0])),
        ),
        (jnp.int32(1), start),
    )[1]
    first_one, first_two = [gather.rows() for gather in attend_gathers]
    value_zero = first_two[:, :blocks]
    leave_zero = first_two[:, blocks : 2 * blocks]
    start = reordered(start.astype(low)).reshape(2, half, width)

    row_places = jnp.concatenate(
        [part * half + jnp.arange(half), (1 - part) * half + jnp.arange(half)]
    )
    spots_group = lax.dynamic_index_in_dim(
        spots_all.reshape(groups, parts, spot_share), group, 0, False
    )
    spots_group = spots_group.reshape(-1)
    encoder_mask = row_places[None, :] < source_lengths[0]
    decoder_mask = (row_places[None, :] <= spots_group[:, None]) & (
        row_places[None, :] < target_lengths[0]
    )
    scored_row = spots_group[:, None] == row_places[None, :]
    heads = ((0, 0), (0, blocks), (1, 0))
    enc_start = start[0] + flipped(first_two[:, 2 * blocks :]).astype(jnp.float32)
    enc_rows = spread(norm_rows(enc_start, gains[0]).astype(low))
    enc_pair = meet(low_product(enc_rows, first_one), late_gathers)
    advance(late_gathers)
    enc_arrays = (enc_pair, low_product(enc_rows, value_zero))
    enc_mixed = attend_forward(enc_arrays, heads, blocks, encoder_mask)
    enc_mixed = meet(enc_mixed, late_gathers)
    advance(late_gathers)
    stream = enc_start + collect(product_nt(enc_mixed, leave_zero))

    feed_rows = meet(norm_rows(stream, gains[1]).astype(low), late_gathers)
    advance(late_gathers)
    feed_rows = spread(feed_rows)
    feed_inner = product(feed_rows, expand_zero)
    feed_hidden = gelu_exact(feed_inner).astype(low)
    after_feed = stream + collect(product_nt(feed_hidden, shrink_zero))
    memory = norm_rows(after_feed, gains[2]).astype(low)

    split = ((0, 0), (1, 0), (1, blocks))
    memory = spread(meet(memory, late_gathers))
    self_weights, cross_weights = [gather.rows() for gather in late_gathers]
    self_query = self_weights[:, :blocks]
    self_keyval = self_weights[:, blocks : 3 * blocks]
    self_leave_weight = self_weights[:, 3 * blocks : 4 * blocks]
    dec_start = start[1] + flipped(self_weights[:, 4 * blocks :]).astype(jnp.float32)
    target_rows = spread(dec_start)
    dec_source = norm_rows(target_rows, gains[3]).astype(low)
    dec_rows = pick_rows(scored_row.astype(low), dec_source)
    dec_arrays = (low_product(dec_rows, self_query), low_product(dec_source, self_keyval))
    dec_mixed = attend_forward(dec_arrays, split, blocks, decoder_mask)
    after_self = place_exact(scored_row, target_rows) + both(
        product_nt(dec_mixed, self_leave_weight)
    )

    cross_query_weight = cross_weights[:, :blocks]
    cross_keyval_weight = cross_weights[:, blocks : 3 * blocks]
    cross_leave_weight = cross_weights[:, 3 * blocks :]
    cross_rows = norm_rows(after_self, gains[4]).astype(low)
    cross_rows, last_weights = tie(cross_rows, feed_weights[1])
    cross_arrays = (
        low_product(cross_rows, cross_query_weight),
        low_product(memory, cross_keyval_weight),
    )
    cross_mixed = attend_forward(cross_arrays, split, blocks, encoder_mask)
    after_cross = after_self + both(product_nt(cross_mixed, cross_leave_weight))

    after_cross = reordered_exact(after_cross)
    expand_one, shrink_one = last_weights[0], last_weights[1]
    last_rows = norm_rows(after_cross, norm_gains[5]).astype(low)
    last_inner = product(last_rows, expand_one)
    last_hidden = gelu_exact(last_inner).astype(low)
    after_last = after_cross + both(product_nt(last_hidden, shrink_one))
    final = norm_rows(after_last, norm_gains[6]).astype(low)

    picked_group = to_all(own_half(final), "dp")
    picked = in_order(picked_group.reshape(-1, width))

    def cores_first(values):
        return jnp.swapaxes(values.reshape(groups, parts, spot_share), 0, 1).reshape(-1)

    label_row = cores_first(labels_all) - (group * parts + part) * rows_owned
    valid = cores_first(valid_all).astype(jnp.float32)
    count = jnp.sum(valid)
    scored_half = picked.shape[0] // 2
    logits = product_nt(picked, own_table)
    onehot = chosen_rows(label_row, rows_owned, jnp.bool_)
    highest = jnp.max(logits, axis=-1)
    log_here = highest + jnp.log(jnp.sum(jnp.exp(logits - highest[:, None]), axis=-1))
    golden_here = jnp.sum(jnp.where(onehot, logits, 0.0), axis=-1)
    stats = to_all(jnp.stack([log_here, golden_here]))
    top = jnp.max(stats[:, 0], axis=0)
    log_total = top + jnp.log(jnp.sum(jnp.exp(stats[:, 0] - top[None]), axis=0))
    golden = jnp.sum(stats[:, 1], axis=0)
    losses = (log_total - golden) * valid
    mean_loss = jnp.sum(losses) / count
    of_group = (pair_order == group).astype(jnp.float32)
    pair_rows = jnp.sum(
        losses.reshape(parts, groups, spot_share) * of_group[None, :, None], axis=1
    )
    pair_losses = jnp.where(part == 0, pair_rows[0], pair_rows[1])[None]
    probs = jnp.exp(logits - log_total[:, None])
    grad_logits = (
        (probs - onehot.astype(jnp.float32)) * (valid / count)[:, None]
    ).astype(low)
    grad_picked = product(grad_logits, own_table)
    kept = own_half(grad_picked)
    sent = jnp.where(part == 0, grad_picked[scored_half:], grad_picked[:scored_half])
    grad_picked = lax.all_to_all(
        (kept + swap(sent)).astype(low).reshape(groups, spot_share, width),
        "dp",
        0,
        0,
        tiled=True,
    )
    grad_final = in_order(jnp.sum(grad_picked.astype(jnp.float32), axis=0))
    grad_table = product_tn(grad_logits, picked)

    grad_rows, gain_six = norm_backward_shared(after_last, norm_gains[6], grad_final)
    grad_low = grad_rows.astype(low)
    last_grads = [low_grad(grad_low, last_hidden)]
    grad_inner = gelu_backward(last_inner, product(grad_low, shrink_one).astype(low))
    last_grads = lax.psum_scatter(
        jnp.stack([low_grad(last_rows, grad_inner)] + last_grads),
        "dp",
        scatter_dimension=1,
        tiled=True,
    ).astype(jnp.float32)
    grad_values, gain_five = norm_backward_shared(
        after_cross, norm_gains[5], both(product_nt(grad_inner, expand_one))
    )
    grad_rows = reordered_exact(grad_rows + grad_values)

    grad_low = grad_rows.astype(low)
    cross_leave = low_grad(grad_low, cross_mixed)
    grad_mixed = low_product(grad_low, cross_leave_weight)
    grad_query, grad_keyval = attend_backward(
        cross_arrays, split, blocks, grad_mixed, encoder_mask
    )
    cross_scatters = [
        Scatter(beside(low_grad(cross_rows, grad_query), cross_leave), 0),
        Scatter(low_grad(memory, grad_keyval), 1),
    ]
    advance(cross_scatters)
    back_source = product_nt(grad_keyval, cross_keyval_weight)
    back_rows = product_nt(grad_query, cross_query_weight)
    grad_stream, gain_two = norm_backward(after_feed, gains[2], collect(back_source))

    grad_all = spread(grad_stream.astype(low))
    grad_inner = gelu_backward(feed_inner, product(grad_all, shrink_zero).astype(low))
    feed_scatters = [Scatter(low_grad(grad_all, feed_hidden), 0)]
    feed_scatters.append(Scatter(low_grad(feed_rows, grad_inner), 1))
    advance(feed_scatters)
    back = product_nt(grad_inner, expand_zero)
    back, back_rows = tie(back, back_rows)
    grad_values, gain_one = norm_backward(stream, gains[1], collect(back))
    grad_stream = grad_stream + grad_values

    grad_values, gain_four = norm_backward_shared(after_self, gains[4], both(back_rows))
    grad_rows = grad_rows + grad_values
    grad_low = grad_rows.astype(low)
    self_leave = low_grad(grad_low, dec_mixed)
    grad_mixed = low_product(grad_low, self_leave_weight)
    grad_query, grad_keyval = attend_backward(
        dec_arrays, split, blocks, grad_mixed, decoder_mask
    )
    self_scatters = [
        Scatter(beside(low_grad(dec_rows, grad_query), self_leave), 0),
        Scatter(low_grad(dec_source, grad_keyval), 1),
    ]
    advance(self_scatters)
    back_source = product_nt(grad_keyval, self_keyval) + place_exact(
        scored_row.T, product_nt(grad_query, self_query)
    )
    grad_decoded, gain_three = norm_backward(dec_start, gains[3], collect(back_source))
    grad_decoded = grad_decoded + place_exact(scored_row[:, :half].T, grad_rows)
    start_decoded = grad_decoded.astype(low)

    grad_all = meet(grad_stream.astype(low), cross_scatters + feed_scatters)
    early = [joined([cross_scatters[b], feed_scatters[b]]) for b in range(2)]
    advance(early)
    grad_all = spread(grad_all)
    grad_mixed = low_product(grad_all, leave_zero)
    first_scatters = [
        Scatter(beside(low_grad(grad_all, enc_mixed), flipped(start_decoded)), 0)
    ]
    advance(first_scatters)
    grad_pair, grad_value = attend_backward(enc_arrays, heads, blocks, grad_mixed, encoder_mask)
    grad_pair = meet(grad_pair, early)
    advance(early)
    back = product_nt(grad_pair, first_one) + product_nt(grad_value, value_zero)
    first_scatters += [
        Scatter(low_grad(enc_rows, grad_pair), 1),
        Scatter(low_grad(enc_rows, grad_value), 0),
    ]
    advance(first_scatters[1:])
    grad_values, gain_zero = norm_backward(enc_start, gains[0], collect(back))
    start_stream = (grad_stream + grad_values).astype(low)
    first_scatters.append(Scatter(flipped(start_stream), 1))

    start_rows = reordered(jnp.concatenate([start_stream, start_decoded])).astype(low)

    def returned(slot):
        return answer(product_tn(chosen_rows(slot, slots_all), start_rows).astype(low))

    def placed(asked, got):
        return product_tn(chosen_rows(asked, rows_owned), got)

    got = returned(slot_in(0))
    advance(first_scatters[3:])
    late = [
        joined([self_scatters[0], first_scatters[0], first_scatters[2]]),
        joined([self_scatters[1], first_scatters[1], first_scatters[3]]),
    ]
    advance(early)
    advance(late)
    got = meet(got, early + late)
    early_rows = [scatter.rows() for scatter in early]
    late_rows = [scatter.rows() for scatter in late]
    table_grad = grad_table + placed(asked_first, got)
    table_grad = lax.while_loop(
        lambda state: state[0] < rounds_all,
        lambda state: (
            state[0] + 1,
            state[1] + placed(ask_again(state[0]), returned(slot_in(state[0]))),
        ),
        (jnp.int32(1), table_grad),
    )[1]

    gain_partial = jnp.concatenate(
        [
            reordered_exact(jnp.stack([gain_zero, gain_one, gain_two, gain_three, gain_four])),
            jnp.stack([gain_five, gain_six]),
        ]
    )
    gain_own = jnp.sum(
        lax.all_to_all(gain_partial.reshape(devices, -1), EVERY, 0, 0, tiled=True), axis=0
    )
    def attention_grads(outer, keyval):
        return [outer[:, :blocks], keyval[:, :blocks], keyval[:, blocks:], outer[:, blocks:]]

    cross_pieces = attention_grads(*[rows[:, : 2 * blocks] for rows in early_rows])
    shrink_rows, expand_rows = [rows[:, 2 * blocks :] for rows in early_rows]
    self_pieces = attention_grads(*[rows[:, : 2 * blocks] for rows in late_rows])
    first_leave, decoded_place, first_value = jnp.split(
        late_rows[0][:, 2 * blocks :], [blocks, blocks + half], axis=1
    )
    first_pieces = pieces_of(late_rows[1], 2 * blocks, 2) + [first_value, first_leave]
    stream_place = late_rows[1][:, 4 * blocks :]
    entry_grad = jnp.stack(
        [jnp.stack(pieces[:3]) for pieces in (first_pieces, self_pieces, cross_pieces)]
    )
    leave_grad = flipped(jnp.stack([first_pieces[3], self_pieces[3], cross_pieces[3]]))
    expand_grad = jnp.stack([expand_rows, last_grads[0]])
    shrink_grad = flipped(jnp.stack([shrink_rows, last_grads[1]]))
    place_grad = flipped(jnp.stack([stream_place, decoded_place]))
    squares = jnp.sum(gain_own * gain_own)
    for grad in (entry_grad, leave_grad, expand_grad, shrink_grad, table_grad, place_grad):
        squares = squares + jnp.sum(grad * grad)
    last_words = to_all(jnp.concatenate([gain_own, squares[None]]))
    gain_grad = last_words[:, :-1].reshape(norm_gains.shape)
    gradient_norm = jnp.sqrt(jnp.sum(last_words[:, -1]))
    clip = jnp.minimum(1.0, MAX_NORM / (gradient_norm + 1e-06))
    steps = step_count[0].astype(jnp.float32)
    fix_one = 1 - FIRST_DECAY**steps
    fix_two = 1 - SECOND_DECAY**steps
    masters = (
        entry_weight,
        exit_weight,
        expand_weight,
        reduce_weight,
        norm_gains,
        token_table,
        place_table,
    )
    firsts = (
        entry_first,
        exit_first,
        expand_first,
        reduce_first,
        gains_first,
        table_first,
        place_first,
    )
    seconds = (
        entry_second,
        exit_second,
        expand_second,
        reduce_second,
        gains_second,
        table_second,
        place_second,
    )
    grads = (entry_grad, leave_grad, expand_grad, shrink_grad, gain_grad, table_grad, place_grad)
    rates = (LEARN_RATE, LEARN_RATE, LEARN_RATE, LEARN_RATE, GAIN_RATE, LEARN_RATE, LEARN_RATE)
    results = [mean_loss, gradient_norm, pair_losses]
    for master, first, second, grad, rate in zip(masters, firsts, seconds, grads, rates):
        results.extend(adam_step(master, first, second, grad, clip, fix_one, fix_two, rate))
    return tuple(results)


def solution(mesh):
    return jax.shard_map(
        local,
        mesh=mesh,
        in_specs=(
            P("dp", "tensor"),
            P("dp", "tensor"),
            P("dp", "tensor"),
            P("dp", "tensor"),
            P("dp"),
            P("dp"),
            P(),
            P(),
            P(None, None, "dp", "tensor"),
            P(None, None, "dp", "tensor"),
            P(None, None, "dp", "tensor"),
            P(None, "tensor", "dp"),
            P(None, "tensor", "dp"),
            P(None, "tensor", "dp"),
            P(None, "dp", "tensor"),
            P(None, "dp", "tensor"),
            P(None, "dp", "tensor"),
            P(None, "tensor", "dp"),
            P(None, "tensor", "dp"),
            P(None, "tensor", "dp"),
            P(),
            P(),
            P(),
            P(("dp", "tensor"), None),
            P(("dp", "tensor"), None),
            P(("dp", "tensor"), None),
            P(None, "tensor", "dp"),
            P(None, "tensor", "dp"),
            P(None, "tensor", "dp"),
        ),
        out_specs=(
            P(),
            P(),
            P("dp", "tensor"),
            P(None, None, "dp", "tensor"),
            P(None, None, "dp", "tensor"),
            P(None, None, "dp", "tensor"),
            P(None, "tensor", "dp"),
            P(None, "tensor", "dp"),
            P(None, "tensor", "dp"),
            P(None, "dp", "tensor"),
            P(None, "dp", "tensor"),
            P(None, "dp", "tensor"),
            P(None, "tensor", "dp"),
            P(None, "tensor", "dp"),
            P(None, "tensor", "dp"),
            P(),
            P(),
            P(),
            P(("dp", "tensor"), None),
            P(("dp", "tensor"), None),
            P(("dp", "tensor"), None),
            P(None, "tensor", "dp"),
            P(None, "tensor", "dp"),
            P(None, "tensor", "dp"),
        ),
        check_vma=False,
    )
```

```python
import functools

import jax
import jax.numpy as jnp
from jax import lax
from jax.experimental import pallas as pl
from jax.experimental.pallas import tpu as pltpu
from jax.sharding import PartitionSpec as P

HEAD_DIM = 64
MAX_NORM = 0.01
LEARN_RATE = 0.03
GAIN_RATE = 0.3
FIRST_DECAY = 0.9
SECOND_DECAY = 0.999
ADAM_EPSILON = 1e-08
WEIGHT_DECAY = 0.01
SCORE_FLOOR = -1000000000.0
EVERY = ("dp", "tensor")
CORE_SWAP = ((0, 1), (1, 0))
SLOTS = 32


def norm_rows(values, gain):
    centered = values - jnp.mean(values, axis=-1, keepdims=True)
    variance = jnp.mean(centered * centered, axis=-1, keepdims=True)
    return centered * lax.rsqrt(variance + 1e-05) * gain


def swap(values):
    return lax.ppermute(values, "tensor", CORE_SWAP)


def spread(rows):
    return jnp.concatenate([rows, swap(rows)], axis=0)


def collect(partial_rows):
    half = partial_rows.shape[0] // 2
    return partial_rows[:half] + swap(partial_rows[half:])


def to_all(values, axis=EVERY):
    size = lax.axis_size(axis)
    return lax.all_to_all(
        jnp.broadcast_to(values[None], (size,) + values.shape), axis, 0, 0, tiled=True
    )


def product(left, right):
    return jnp.dot(left, right, preferred_element_type=jnp.float32)


def product_tn(left, right):
    return lax.dot_general(
        left, right, (((0,), (0,)), ((), ())), preferred_element_type=jnp.float32
    )


def product_nt(left, right):
    return lax.dot_general(
        left, right, (((1,), (1,)), ((), ())), preferred_element_type=jnp.float32
    )


def attend_forward_kernel(places, width, *refs):
    allowed_ref, mixed_ref = refs[-2:]
    allowed = allowed_ref[...] > 0
    for first in range(0, width, HEAD_DIM):
        query, key, value = [
            refs[ref][:, start + first : start + first + HEAD_DIM] for ref, start in places
        ]
        scores = jnp.where(allowed, product_nt(query, key) * HEAD_DIM ** (-0.5), SCORE_FLOOR)
        powers = jnp.exp(scores - jnp.max(scores, axis=1, keepdims=True))
        weights = powers * (1.0 / jnp.sum(powers, axis=1, keepdims=True))
        mixed = product(weights.astype(jnp.bfloat16), value)
        mixed_ref[:, first : first + HEAD_DIM] = mixed.astype(jnp.bfloat16)


def attend_backward_kernel(places, width, *refs):
    count = (len(refs) - 2) // 2
    grad_ref, allowed_ref = refs[count : count + 2]
    out_refs = refs[count + 2 :]
    allowed = allowed_ref[...] > 0
    for first in range(0, width, HEAD_DIM):
        query, key, value = [
            refs[ref][:, start + first : start + first + HEAD_DIM] for ref, start in places
        ]
        grad = grad_ref[:, first : first + HEAD_DIM]
        scores = jnp.where(allowed, product_nt(key, query) * HEAD_DIM ** (-0.5), SCORE_FLOOR)
        powers = jnp.exp(scores - jnp.max(scores, axis=0, keepdims=True))
        weights = powers * (1.0 / jnp.sum(powers, axis=0, keepdims=True))
        grad_value = product(weights.astype(jnp.bfloat16), grad)
        grad_weights = product_nt(value, grad)
        inner = jnp.sum(weights * grad_weights, axis=0, keepdims=True)
        grad_scores = (weights * (grad_weights - inner) * HEAD_DIM ** (-0.5)).astype(jnp.bfloat16)
        grads = (product_tn(grad_scores, key), product(grad_scores, query), grad_value)
        for (ref, start), values in zip(places, grads):
            out_refs[ref][:, start + first : start + first + HEAD_DIM] = values.astype(jnp.bfloat16)


def kernel_call(kernel, outputs, operands, flops):
    size = sum(value.size * value.dtype.itemsize for value in operands)
    return pl.pallas_call(
        kernel,
        out_shape=outputs,
        in_specs=[pl.BlockSpec(memory_space=pltpu.VMEM)] * len(operands),
        out_specs=jax.tree.map(lambda _: pl.BlockSpec(memory_space=pltpu.VMEM), outputs),
        compiler_params=pltpu.CompilerParams(vmem_limit_bytes=32 * 1024 * 1024),
        cost_estimate=pl.CostEstimate(flops=flops, bytes_accessed=2 * size, transcendentals=0),
    )(*operands)


def attend_forward(arrays, places, width, allowed):
    rows = arrays[places[0][0]].shape[0]
    return kernel_call(
        functools.partial(attend_forward_kernel, places, width),
        jax.ShapeDtypeStruct((rows, width), jnp.bfloat16),
        arrays + (allowed.astype(jnp.float32),),
        16 * rows * width * arrays[places[1][0]].shape[0],
    )


def attend_backward(arrays, places, width, grad_mixed, allowed):
    rows = grad_mixed.shape[0]
    return kernel_call(
        functools.partial(attend_backward_kernel, places, width),
        tuple(jax.ShapeDtypeStruct(array.shape, array.dtype) for array in arrays),
        arrays + (grad_mixed, allowed.astype(jnp.float32).T),
        40 * rows * width * arrays[places[1][0]].shape[0],
    )


def pick_rows(index, rows):
    return product(index, rows).astype(jnp.bfloat16)


def place_exact(index, rows):
    return jnp.dot(
        index.astype(jnp.float32),
        rows,
        precision=lax.Precision.HIGHEST,
        preferred_element_type=jnp.float32,
    )


def both(partial_rows):
    return partial_rows + swap(partial_rows)


def norm_backward(values, gain, grad):
    grad_values, grad_gain = jax.vjp(norm_rows, values, gain)[1](grad)
    return grad_values, grad_gain


def own_half(rows):
    half = rows.shape[0] // 2
    return jnp.where(lax.axis_index("tensor") == 0, rows[:half], rows[half:])


def in_order(rows):
    other = swap(rows)
    return jnp.where(
        lax.axis_index("tensor") == 0,
        jnp.concatenate([rows, other]),
        jnp.concatenate([other, rows]),
    )


def norm_backward_shared(values, gain, grad):
    grad_values = jax.vjp(lambda rows: norm_rows(rows, gain), values)[1](grad)[0]
    own = own_half(values)
    grad_gain = jax.vjp(lambda scale: norm_rows(own, scale), gain)[1](own_half(grad))[0]
    return grad_values, grad_gain


def tie(*values):
    return lax.optimization_barrier(values)


def low_grad(left, right):
    return product_tn(left, right).astype(jnp.bfloat16)


def low_product(left, right):
    return product(left, right).astype(jnp.bfloat16)


def gelu_exact(values):
    return jax.nn.gelu(values, approximate=False)


def gelu_backward(inner, grad_hidden):
    return jax.vjp(gelu_exact, inner)[1](grad_hidden.astype(jnp.float32))[0].astype(jnp.bfloat16)


def adam_step(master, first, second, grad, clip, fix_one, fix_two, rate):
    grad = grad * clip
    first_new = FIRST_DECAY * first + (1 - FIRST_DECAY) * grad
    second_new = SECOND_DECAY * second + (1 - SECOND_DECAY) * grad * grad
    master_new = master - rate * (
        first_new / fix_one / (jnp.sqrt(second_new / fix_two) + ADAM_EPSILON)
        + WEIGHT_DECAY * master
    )
    return (master_new, first_new, second_new)


def bit_order(turn):
    count = (lax.axis_size("dp") - 1).bit_length()
    order = list(range(count - 1, -1, -1))
    if turn % 2:
        for first in range(0, count - 1, 2):
            order[first], order[first + 1] = order[first + 1], order[first]
    return order


def swap_bit(values, bit):
    pairs = [(group, group ^ (1 << bit)) for group in range(lax.axis_size("dp"))]
    return lax.ppermute(values, "dp", pairs)


class Gather:
    def __init__(self, shard, turn):
        self.held, self.got = shard[None], None
        self.order = bit_order(turn)
        self.bits = []

    def settle(self):
        if self.got is None:
            return
        bit = self.order[len(self.bits)]
        block = self.held.shape[1:]
        above = sum(1 for other in self.bits if other > bit)
        shape = (2**above, 2 ** (len(self.bits) - above)) + block
        held = jnp.stack([self.held.reshape(shape), self.got.reshape(shape)], axis=1)
        self.held, self.got = held.reshape((-1,) + block), None
        self.bits.append(bit)

    def step(self):
        self.settle()
        self.got = swap_bit(self.held, self.order[len(self.bits)])

    def left(self):
        return len(self.order) - len(self.bits) - (self.got is not None)

    def rows(self):
        while self.left():
            self.step()
        self.settle()
        return self.held.reshape(-1, self.held.shape[2])


class Scatter:
    def __init__(self, grads, turn):
        groups = lax.axis_size("dp")
        self.held = grads.reshape((groups, grads.shape[0] // groups, grads.shape[1]))
        self.got = None
        self.order = bit_order(turn)
        self.bits = sorted(self.order, reverse=True)

    def settle(self):
        if self.got is not None:
            held = self.held.astype(jnp.float32) + self.got.astype(jnp.float32)
            self.held, self.got = held.reshape((-1,) + held.shape[2:]), None

    def step(self):
        self.settle()
        bit = self.order.pop()
        above = self.bits.index(bit)
        halves = self.held.reshape((2**above, 2, -1) + self.held.shape[1:])
        self.got = swap_bit(halves[:, 1].astype(jnp.bfloat16), bit)
        self.held = halves[:, 0]
        self.bits.remove(bit)

    def left(self):
        return len(self.order)

    def rows(self):
        while self.left():
            self.step()
        self.settle()
        return self.held[0]


def joined(scatters):
    whole = Scatter(jnp.zeros((lax.axis_size("dp"), 1)), 0)
    for scatter in scatters:
        scatter.settle()
    whole.held = jnp.concatenate([scatter.held for scatter in scatters], axis=2)
    whole.order, whole.bits = list(scatters[0].order), list(scatters[0].bits)
    return whole


def advance(movers):
    for mover in movers:
        if mover.left():
            mover.step()


def meet(value, movers):
    sent = [mover for mover in movers if mover.got is not None]
    tied = tie(value, *[mover.got for mover in sent])
    for mover, got in zip(sent, tied[1:]):
        mover.got = got
    return tied[0]


def flipped(values):
    return jnp.swapaxes(values, -1, -2)


def request_slots(ids, rows_owned):
    owner = ids // rows_owned
    here = jnp.arange(ids.shape[0])
    earlier = here[None, :] < here[:, None]
    same = ids[:, None] == ids[None, :]
    leads = jnp.sum((same & earlier).astype(jnp.int32), axis=1) == 0
    leader = jnp.min(jnp.where(same, here[None, :], ids.shape[0]), axis=1)
    rank = jnp.sum(
        (
            (here[None, :] < leader[:, None])
            & leads[None, :]
            & (owner[:, None] == owner[None, :])
        ).astype(jnp.int32),
        axis=1,
    )
    return owner, rank, leads


def chosen_rows(index, count, dtype=jnp.bfloat16):
    return (index[:, None] == jnp.arange(count)[None, :]).astype(dtype)


def local(
    source_ids,
    target_ids,
    score_places,
    target_labels,
    source_lengths,
    target_lengths,
    pair_order,
    step_count,
    entry_weight,
    entry_first,
    entry_second,
    exit_weight,
    exit_first,
    exit_second,
    expand_weight,
    expand_first,
    expand_second,
    reduce_weight,
    reduce_first,
    reduce_second,
    norm_gains,
    gains_first,
    gains_second,
    token_table,
    table_first,
    table_second,
    place_table,
    place_first,
    place_second,
):
    groups = lax.axis_size("dp")
    parts = lax.axis_size("tensor")
    devices = groups * parts
    group = lax.axis_index("dp")
    part = lax.axis_index("tensor")
    low = jnp.bfloat16
    rows_owned, width = token_table.shape
    half = source_ids.shape[1]
    spot_share = score_places.shape[1]

    share = width // groups
    feature = jnp.arange(width)
    home = (feature // share ^ group) * share + feature % share
    order = home[:, None] == feature[None, :]

    def reordered(values):
        return product(values, order.astype(low))

    def reordered_exact(values):
        return jnp.dot(
            values,
            order.astype(jnp.float32),
            precision=lax.Precision.HIGHEST,
            preferred_element_type=jnp.float32,
        )

    gains = reordered_exact(norm_gains)
    blocks = entry_weight.shape[3]
    entry_low = entry_weight.astype(low)
    leave_low = flipped(exit_weight.astype(low))
    place_low = flipped(place_table.astype(low))
    expand_low = expand_weight.astype(low)
    shrink_low = flipped(reduce_weight.astype(low))
    wide = expand_low.shape[2]

    def beside(*pieces):
        return jnp.concatenate(pieces, axis=1)

    attend_gathers = [
        Gather(beside(entry_low[0, 0], entry_low[0, 1]), 0),
        Gather(beside(entry_low[0, 2], leave_low[0], place_low[0]), 1),
    ]
    late_gathers = [
        Gather(
            beside(entry_low[1, 0], entry_low[1, 1], entry_low[1, 2], leave_low[1], place_low[1]),
            0,
        ),
        Gather(beside(entry_low[2, 0], entry_low[2, 1], entry_low[2, 2], leave_low[2]), 1),
    ]
    advance(attend_gathers)
    feed_weights = [
        lax.all_gather(jnp.stack([expand_low[b], shrink_low[b]]), "dp", axis=1, tiled=True)
        for b in range(2)
    ]

    def pieces_of(values, first, count):
        return [
            values[:, first + b * blocks : first + (b + 1) * blocks] for b in range(count)
        ]

    ids = jnp.concatenate([source_ids[0], target_ids[0]])
    owner, rank, leads = request_slots(ids, rows_owned)
    rounds = jnp.max(rank) // SLOTS + 1
    slots_all = devices * SLOTS
    slot_names = jnp.arange(slots_all)

    def slot_in(turn):
        return jnp.where(rank // SLOTS == turn, owner * SLOTS + rank % SLOTS, -1)

    def requests_in(turn):
        asked = (slot_names[:, None] == slot_in(turn)[None, :]) & leads[None, :]
        return jnp.sum(
            jnp.where(asked, ids[None, :] % rows_owned + 1, 0), axis=1
        ).reshape(devices, SLOTS)

    spots = score_places[0]
    extras = jnp.concatenate(
        [
            spots,
            target_labels[0],
            (spots < target_lengths[0]).astype(jnp.int32),
            rounds[None],
        ]
    )
    message = jnp.concatenate(
        [
            requests_in(0),
            jnp.broadcast_to(extras[None], (devices, extras.shape[0])),
        ],
        axis=1,
    )
    heard = lax.all_to_all(message, EVERY, 0, 0, tiled=True)
    heard = meet(heard, attend_gathers)
    advance(attend_gathers)
    asked_first = heard[:, :SLOTS].reshape(-1) - 1
    spots_all = heard[:, SLOTS : SLOTS + spot_share]
    labels_all = heard[:, SLOTS + spot_share : SLOTS + 2 * spot_share]
    valid_all = heard[:, SLOTS + 2 * spot_share : SLOTS + 3 * spot_share]
    rounds_all = jnp.max(heard[:, -1])
    own_table = token_table.astype(low)

    def picked_rows(asked):
        return product(chosen_rows(asked, rows_owned), own_table).astype(low)

    def answer(sent):
        return lax.all_to_all(
            sent.reshape(devices, SLOTS, width), EVERY, 0, 0, tiled=True
        ).reshape(slots_all, width)

    def looked_up(got, slot):
        return product(chosen_rows(slot, slots_all), got)

    def ask_again(turn):
        return (
            lax.all_to_all(requests_in(turn), EVERY, 0, 0, tiled=True).reshape(-1) - 1
        )

    asked_rows = meet(picked_rows(asked_first), attend_gathers)
    got = answer(asked_rows)
    advance(attend_gathers)
    late_gathers[0].held, late_gathers[1].held = tie(
        meet(late_gathers[0].held, attend_gathers), late_gathers[1].held
    )
    advance(attend_gathers)
    advance(late_gathers)
    got = meet(got, attend_gathers + late_gathers)
    got, feed_weights[0] = tie(got, feed_weights[0])
    advance(late_gathers)
    expand_zero = pick_rows(order.astype(low), feed_weights[0][0])
    shrink_zero = pick_rows(order.astype(low), feed_weights[0][1])
    start = looked_up(got, slot_in(0))
    start = lax.while_loop(
        lambda state: state[0] < rounds_all,
        lambda state: (
            state[0] + 1,
            state[1] + looked_up(answer(picked_rows(ask_again(state[0]))), slot_in(state[0])),
        ),
        (jnp.int32(1), start),
    )[1]
    first_one, first_two = [gather.rows() for gather in attend_gathers]
    value_zero = first_two[:, :blocks]
    leave_zero = first_two[:, blocks : 2 * blocks]
    start = reordered(start.astype(low)).reshape(2, half, width)

    row_places = jnp.concatenate(
        [part * half + jnp.arange(half), (1 - part) * half + jnp.arange(half)]
    )
    spots_group = lax.dynamic_index_in_dim(
        spots_all.reshape(groups, parts, spot_share), group, 0, False
    )
    spots_group = spots_group.reshape(-1)
    encoder_mask = row_places[None, :] < source_lengths[0]
    decoder_mask = (row_places[None, :] <= spots_group[:, None]) & (
        row_places[None, :] < target_lengths[0]
    )
    scored_row = spots_group[:, None] == row_places[None, :]
    heads = ((0, 0), (0, blocks), (1, 0))
    enc_start = start[0] + flipped(first_two[:, 2 * blocks :]).astype(jnp.float32)
    enc_rows = meet(norm_rows(enc_start, gains[0]).astype(low), late_gathers)
    advance(late_gathers)
    enc_rows = spread(enc_rows)
    enc_pair = low_product(enc_rows, first_one)
    enc_arrays = (enc_pair, low_product(enc_rows, value_zero))
    enc_mixed = attend_forward(enc_arrays, heads, blocks, encoder_mask)
    enc_mixed = meet(enc_mixed, late_gathers)
    advance(late_gathers)
    stream = enc_start + collect(product_nt(enc_mixed, leave_zero))

    feed_rows = spread(norm_rows(stream, gains[1]).astype(low))
    feed_inner = product(feed_rows, expand_zero)
    feed_hidden = meet(gelu_exact(feed_inner).astype(low), late_gathers)
    after_feed = stream + collect(product_nt(feed_hidden, shrink_zero))
    memory = norm_rows(after_feed, gains[2]).astype(low)

    split = ((0, 0), (1, 0), (1, blocks))
    memory = spread(meet(memory, late_gathers))
    self_weights, cross_weights = [gather.rows() for gather in late_gathers]
    self_query = self_weights[:, :blocks]
    self_keyval = self_weights[:, blocks : 3 * blocks]
    self_leave_weight = self_weights[:, 3 * blocks : 4 * blocks]
    dec_start = start[1] + flipped(self_weights[:, 4 * blocks :]).astype(jnp.float32)
    target_rows = spread(dec_start)
    dec_source = norm_rows(target_rows, gains[3]).astype(low)
    dec_rows = pick_rows(scored_row.astype(low), dec_source)
    dec_arrays = (low_product(dec_rows, self_query), low_product(dec_source, self_keyval))
    dec_mixed = attend_forward(dec_arrays, split, blocks, decoder_mask)
    after_self = place_exact(scored_row, target_rows) + both(
        product_nt(dec_mixed, self_leave_weight)
    )

    cross_query_weight = cross_weights[:, :blocks]
    cross_keyval_weight = cross_weights[:, blocks : 3 * blocks]
    cross_leave_weight = cross_weights[:, 3 * blocks :]
    cross_rows = norm_rows(after_self, gains[4]).astype(low)
    cross_rows, last_weights = tie(cross_rows, feed_weights[1])
    cross_arrays = (
        low_product(cross_rows, cross_query_weight),
        low_product(memory, cross_keyval_weight),
    )
    cross_mixed = attend_forward(cross_arrays, split, blocks, encoder_mask)
    after_cross = after_self + both(product_nt(cross_mixed, cross_leave_weight))

    after_cross = reordered_exact(after_cross)
    expand_one, shrink_one = last_weights[0], last_weights[1]
    last_rows = norm_rows(after_cross, norm_gains[5]).astype(low)
    last_inner = product(last_rows, expand_one)
    last_hidden = gelu_exact(last_inner).astype(low)
    after_last = after_cross + both(product_nt(last_hidden, shrink_one))
    final = norm_rows(after_last, norm_gains[6]).astype(low)

    picked_group = to_all(own_half(final), "dp")
    picked = in_order(picked_group.reshape(-1, width))

    def cores_first(values):
        return jnp.swapaxes(values.reshape(groups, parts, spot_share), 0, 1).reshape(-1)

    label_row = cores_first(labels_all) - (group * parts + part) * rows_owned
    valid = cores_first(valid_all).astype(jnp.float32)
    count = jnp.sum(valid)
    scored_half = picked.shape[0] // 2
    logits = product_nt(picked, own_table)
    onehot = chosen_rows(label_row, rows_owned, jnp.bool_)
    highest = jnp.max(logits, axis=-1)
    log_here = highest + jnp.log(jnp.sum(jnp.exp(logits - highest[:, None]), axis=-1))
    golden_here = jnp.sum(jnp.where(onehot, logits, 0.0), axis=-1)
    stats = to_all(jnp.stack([log_here, golden_here]))
    top = jnp.max(stats[:, 0], axis=0)
    log_total = top + jnp.log(jnp.sum(jnp.exp(stats[:, 0] - top[None]), axis=0))
    golden = jnp.sum(stats[:, 1], axis=0)
    losses = (log_total - golden) * valid
    mean_loss = jnp.sum(losses) / count
    of_group = (pair_order == group).astype(jnp.float32)
    pair_rows = jnp.sum(
        losses.reshape(parts, groups, spot_share) * of_group[None, :, None], axis=1
    )
    pair_losses = jnp.where(part == 0, pair_rows[0], pair_rows[1])[None]
    probs = jnp.exp(logits - log_total[:, None])
    grad_logits = (
        (probs - onehot.astype(jnp.float32)) * (valid / count)[:, None]
    ).astype(low)
    grad_picked = product(grad_logits, own_table)
    kept = own_half(grad_picked)
    sent = jnp.where(part == 0, grad_picked[scored_half:], grad_picked[:scored_half])
    grad_picked = lax.all_to_all(
        (kept + swap(sent)).astype(low).reshape(groups, spot_share, width),
        "dp",
        0,
        0,
        tiled=True,
    )
    grad_final = in_order(jnp.sum(grad_picked.astype(jnp.float32), axis=0))
    grad_table = product_tn(grad_logits, picked)

    grad_rows, gain_six = norm_backward_shared(after_last, norm_gains[6], grad_final)
    grad_low = grad_rows.astype(low)
    last_grads = [low_grad(grad_low, last_hidden)]
    grad_inner = gelu_backward(last_inner, product(grad_low, shrink_one).astype(low))
    last_grads = lax.psum_scatter(
        jnp.stack([low_grad(last_rows, grad_inner)] + last_grads),
        "dp",
        scatter_dimension=1,
        tiled=True,
    ).astype(jnp.float32)
    grad_values, gain_five = norm_backward_shared(
        after_cross, norm_gains[5], both(product_nt(grad_inner, expand_one))
    )
    grad_rows = reordered_exact(grad_rows + grad_values)

    grad_low = grad_rows.astype(low)
    cross_leave = low_grad(grad_low, cross_mixed)
    grad_mixed = low_product(grad_low, cross_leave_weight)
    grad_query, grad_keyval = attend_backward(
        cross_arrays, split, blocks, grad_mixed, encoder_mask
    )
    cross_scatters = [
        Scatter(beside(low_grad(cross_rows, grad_query), cross_leave), 0),
        Scatter(low_grad(memory, grad_keyval), 1),
    ]
    advance(cross_scatters)
    back_source = product_nt(grad_keyval, cross_keyval_weight)
    back_rows = product_nt(grad_query, cross_query_weight)
    grad_stream, gain_two = norm_backward(after_feed, gains[2], collect(back_source))

    grad_all = spread(grad_stream.astype(low))
    grad_inner = gelu_backward(feed_inner, product(grad_all, shrink_zero).astype(low))
    feed_scatters = [Scatter(low_grad(grad_all, feed_hidden), 0)]
    feed_scatters.append(Scatter(low_grad(feed_rows, grad_inner), 1))
    advance(feed_scatters)
    back = product_nt(grad_inner, expand_zero)
    back, back_rows = tie(back, back_rows)
    grad_values, gain_one = norm_backward(stream, gains[1], collect(back))
    grad_stream = grad_stream + grad_values

    grad_values, gain_four = norm_backward_shared(after_self, gains[4], both(back_rows))
    grad_rows = grad_rows + grad_values
    grad_low = grad_rows.astype(low)
    self_leave = low_grad(grad_low, dec_mixed)
    grad_mixed = low_product(grad_low, self_leave_weight)
    grad_query, grad_keyval = attend_backward(
        dec_arrays, split, blocks, grad_mixed, decoder_mask
    )
    self_scatters = [
        Scatter(beside(low_grad(dec_rows, grad_query), self_leave), 0),
        Scatter(low_grad(dec_source, grad_keyval), 1),
    ]
    advance(self_scatters)
    back_source = product_nt(grad_keyval, self_keyval) + place_exact(
        scored_row.T, product_nt(grad_query, self_query)
    )
    grad_decoded, gain_three = norm_backward(dec_start, gains[3], collect(back_source))
    grad_decoded = grad_decoded + place_exact(scored_row[:, :half].T, grad_rows)
    start_decoded = grad_decoded.astype(low)

    grad_all = spread(grad_stream.astype(low))
    grad_mixed = low_product(grad_all, leave_zero)
    first_scatters = [
        Scatter(beside(low_grad(grad_all, enc_mixed), flipped(start_decoded)), 0)
    ]
    advance(first_scatters)
    grad_pair, grad_value = attend_backward(enc_arrays, heads, blocks, grad_mixed, encoder_mask)
    grad_pair = meet(grad_pair, cross_scatters + feed_scatters)
    early = [joined([cross_scatters[b], feed_scatters[b]]) for b in range(2)]
    advance(early)
    back = product_nt(grad_pair, first_one) + product_nt(grad_value, value_zero)
    first_scatters += [
        Scatter(low_grad(enc_rows, grad_pair), 1),
        Scatter(low_grad(enc_rows, grad_value), 0),
    ]
    advance(first_scatters[1:])
    grad_values, gain_zero = norm_backward(enc_start, gains[0], collect(back))
    start_stream = (grad_stream + grad_values).astype(low)
    place_scatter = Scatter(flipped(start_stream), 1)
    advance([place_scatter])

    start_rows = reordered(jnp.concatenate([start_stream, start_decoded])).astype(low)

    def returned(slot):
        return answer(product_tn(chosen_rows(slot, slots_all), start_rows).astype(low))

    def placed(asked, got):
        return product_tn(chosen_rows(asked, rows_owned), got)

    got = returned(slot_in(0))
    got = meet(got, early)
    got = meet(got, self_scatters + first_scatters + [place_scatter])
    got, last_grads = tie(got, last_grads)
    late = [
        joined([self_scatters[0], first_scatters[0], first_scatters[2]]),
        joined([self_scatters[1], first_scatters[1], place_scatter]),
    ]
    advance(early)
    advance(late)
    gain_partial = jnp.concatenate(
        [
            reordered_exact(jnp.stack([gain_zero, gain_one, gain_two, gain_three, gain_four])),
            jnp.stack([gain_five, gain_six]),
        ]
    )
    gain_partial, got = tie(gain_partial, got)
    gain_own = jnp.sum(
        lax.all_to_all(gain_partial.reshape(devices, -1), EVERY, 0, 0, tiled=True), axis=0
    )
    table_grad = grad_table + placed(asked_first, got)
    table_grad = lax.while_loop(
        lambda state: state[0] < rounds_all,
        lambda state: (
            state[0] + 1,
            state[1] + placed(ask_again(state[0]), returned(slot_in(state[0]))),
        ),
        (jnp.int32(1), table_grad),
    )[1]
    squares = jnp.sum(table_grad * table_grad)
    squares, gain_own = tie(squares, gain_own)
    squares = meet(squares, early + late)
    advance(early)
    advance(late)
    squares = meet(squares, early + late)
    advance(late)
    early_rows = [scatter.rows() for scatter in early]
    late_rows = [scatter.rows() for scatter in late]
    stream_place = late_rows[1][:, 4 * blocks :]
    def attention_grads(outer, keyval):
        return [outer[:, :blocks], keyval[:, :blocks], keyval[:, blocks:], outer[:, blocks:]]

    cross_pieces = attention_grads(*[rows[:, : 2 * blocks] for rows in early_rows])
    shrink_rows, expand_rows = [rows[:, 2 * blocks :] for rows in early_rows]
    self_pieces = attention_grads(*[rows[:, : 2 * blocks] for rows in late_rows])
    first_leave, decoded_place, first_value = jnp.split(
        late_rows[0][:, 2 * blocks :], [blocks, blocks + half], axis=1
    )
    first_pieces = pieces_of(late_rows[1], 2 * blocks, 2) + [first_value, first_leave]
    entry_grad = jnp.stack(
        [jnp.stack(pieces[:3]) for pieces in (first_pieces, self_pieces, cross_pieces)]
    )
    leave_grad = flipped(jnp.stack([first_pieces[3], self_pieces[3], cross_pieces[3]]))
    expand_grad = jnp.stack([expand_rows, last_grads[0]])
    shrink_grad = flipped(jnp.stack([shrink_rows, last_grads[1]]))
    place_grad = flipped(jnp.stack([stream_place, decoded_place]))
    squares = squares + jnp.sum(gain_own * gain_own)
    for grad in (entry_grad, leave_grad, expand_grad, shrink_grad, place_grad):
        squares = squares + jnp.sum(grad * grad)
    last_words = to_all(jnp.concatenate([gain_own, squares[None]]))
    gain_grad = last_words[:, :-1].reshape(norm_gains.shape)
    gradient_norm = jnp.sqrt(jnp.sum(last_words[:, -1]))
    clip = jnp.minimum(1.0, MAX_NORM / (gradient_norm + 1e-06))
    steps = step_count[0].astype(jnp.float32)
    fix_one = 1 - FIRST_DECAY**steps
    fix_two = 1 - SECOND_DECAY**steps
    masters = (
        entry_weight,
        exit_weight,
        expand_weight,
        reduce_weight,
        norm_gains,
        token_table,
        place_table,
    )
    firsts = (
        entry_first,
        exit_first,
        expand_first,
        reduce_first,
        gains_first,
        table_first,
        place_first,
    )
    seconds = (
        entry_second,
        exit_second,
        expand_second,
        reduce_second,
        gains_second,
        table_second,
        place_second,
    )
    grads = (entry_grad, leave_grad, expand_grad, shrink_grad, gain_grad, table_grad, place_grad)
    rates = (LEARN_RATE, LEARN_RATE, LEARN_RATE, LEARN_RATE, GAIN_RATE, LEARN_RATE, LEARN_RATE)
    results = [mean_loss, gradient_norm, pair_losses]
    for master, first, second, grad, rate in zip(masters, firsts, seconds, grads, rates):
        results.extend(adam_step(master, first, second, grad, clip, fix_one, fix_two, rate))
    return tuple(results)


def solution(mesh):
    return jax.shard_map(
        local,
        mesh=mesh,
        in_specs=(
            P("dp", "tensor"),
            P("dp", "tensor"),
            P("dp", "tensor"),
            P("dp", "tensor"),
            P("dp"),
            P("dp"),
            P(),
            P(),
            P(None, None, "dp", "tensor"),
            P(None, None, "dp", "tensor"),
            P(None, None, "dp", "tensor"),
            P(None, "tensor", "dp"),
            P(None, "tensor", "dp"),
            P(None, "tensor", "dp"),
            P(None, "dp", "tensor"),
            P(None, "dp", "tensor"),
            P(None, "dp", "tensor"),
            P(None, "tensor", "dp"),
            P(None, "tensor", "dp"),
            P(None, "tensor", "dp"),
            P(),
            P(),
            P(),
            P(("dp", "tensor"), None),
            P(("dp", "tensor"), None),
            P(("dp", "tensor"), None),
            P(None, "tensor", "dp"),
            P(None, "tensor", "dp"),
            P(None, "tensor", "dp"),
        ),
        out_specs=(
            P(),
            P(),
            P("dp", "tensor"),
            P(None, None, "dp", "tensor"),
            P(None, None, "dp", "tensor"),
            P(None, None, "dp", "tensor"),
            P(None, "tensor", "dp"),
            P(None, "tensor", "dp"),
            P(None, "tensor", "dp"),
            P(None, "dp", "tensor"),
            P(None, "dp", "tensor"),
            P(None, "dp", "tensor"),
            P(None, "tensor", "dp"),
            P(None, "tensor", "dp"),
            P(None, "tensor", "dp"),
            P(),
            P(),
            P(),
            P(("dp", "tensor"), None),
            P(("dp", "tensor"), None),
            P(("dp", "tensor"), None),
            P(None, "tensor", "dp"),
            P(None, "tensor", "dp"),
            P(None, "tensor", "dp"),
        ),
        check_vma=False,
    )
```

```python
import functools

import jax
import jax.numpy as jnp
from jax import lax
from jax.experimental import pallas as pl
from jax.experimental.pallas import tpu as pltpu
from jax.sharding import PartitionSpec as P

HEAD_DIM = 64
MAX_NORM = 0.01
LEARN_RATE = 0.03
GAIN_RATE = 0.3
FIRST_DECAY = 0.9
SECOND_DECAY = 0.999
ADAM_EPSILON = 1e-08
WEIGHT_DECAY = 0.01
SCORE_FLOOR = -1000000000.0
EVERY = ("dp", "tensor")
CORE_SWAP = ((0, 1), (1, 0))
SLOTS = 32


def norm_rows(values, gain):
    centered = values - jnp.mean(values, axis=-1, keepdims=True)
    variance = jnp.mean(centered * centered, axis=-1, keepdims=True)
    return centered * lax.rsqrt(variance + 1e-05) * gain


def swap(values):
    return lax.ppermute(values, "tensor", CORE_SWAP)


def spread(rows):
    return jnp.concatenate([rows, swap(rows)], axis=0)


def collect(partial_rows):
    half = partial_rows.shape[0] // 2
    return partial_rows[:half] + swap(partial_rows[half:])


def to_all(values, axis=EVERY):
    size = lax.axis_size(axis)
    return lax.all_to_all(
        jnp.broadcast_to(values[None], (size,) + values.shape), axis, 0, 0, tiled=True
    )


def product(left, right):
    return jnp.dot(left, right, preferred_element_type=jnp.float32)


def product_tn(left, right):
    return lax.dot_general(
        left, right, (((0,), (0,)), ((), ())), preferred_element_type=jnp.float32
    )


def product_nt(left, right):
    return lax.dot_general(
        left, right, (((1,), (1,)), ((), ())), preferred_element_type=jnp.float32
    )


def attend_forward_kernel(places, width, *refs):
    allowed_ref, mixed_ref = refs[-2:]
    allowed = allowed_ref[...] > 0
    for first in range(0, width, HEAD_DIM):
        query, key, value = [
            refs[ref][:, start + first : start + first + HEAD_DIM] for ref, start in places
        ]
        scores = jnp.where(allowed, product_nt(query, key) * HEAD_DIM ** (-0.5), SCORE_FLOOR)
        powers = jnp.exp(scores - jnp.max(scores, axis=1, keepdims=True))
        weights = powers * (1.0 / jnp.sum(powers, axis=1, keepdims=True))
        mixed = product(weights.astype(jnp.bfloat16), value)
        mixed_ref[:, first : first + HEAD_DIM] = mixed.astype(jnp.bfloat16)


def attend_backward_kernel(places, width, *refs):
    count = (len(refs) - 2) // 2
    grad_ref, allowed_ref = refs[count : count + 2]
    out_refs = refs[count + 2 :]
    allowed = allowed_ref[...] > 0
    for first in range(0, width, HEAD_DIM):
        query, key, value = [
            refs[ref][:, start + first : start + first + HEAD_DIM] for ref, start in places
        ]
        grad = grad_ref[:, first : first + HEAD_DIM]
        scores = jnp.where(allowed, product_nt(key, query) * HEAD_DIM ** (-0.5), SCORE_FLOOR)
        powers = jnp.exp(scores - jnp.max(scores, axis=0, keepdims=True))
        weights = powers * (1.0 / jnp.sum(powers, axis=0, keepdims=True))
        grad_value = product(weights.astype(jnp.bfloat16), grad)
        grad_weights = product_nt(value, grad)
        inner = jnp.sum(weights * grad_weights, axis=0, keepdims=True)
        grad_scores = (weights * (grad_weights - inner) * HEAD_DIM ** (-0.5)).astype(jnp.bfloat16)
        grads = (product_tn(grad_scores, key), product(grad_scores, query), grad_value)
        for (ref, start), values in zip(places, grads):
            out_refs[ref][:, start + first : start + first + HEAD_DIM] = values.astype(jnp.bfloat16)


def kernel_call(kernel, outputs, operands, flops):
    size = sum(value.size * value.dtype.itemsize for value in operands)
    return pl.pallas_call(
        kernel,
        out_shape=outputs,
        in_specs=[pl.BlockSpec(memory_space=pltpu.VMEM)] * len(operands),
        out_specs=jax.tree.map(lambda _: pl.BlockSpec(memory_space=pltpu.VMEM), outputs),
        compiler_params=pltpu.CompilerParams(vmem_limit_bytes=32 * 1024 * 1024),
        cost_estimate=pl.CostEstimate(flops=flops, bytes_accessed=2 * size, transcendentals=0),
    )(*operands)


def attend_forward(arrays, places, width, allowed):
    rows = arrays[places[0][0]].shape[0]
    return kernel_call(
        functools.partial(attend_forward_kernel, places, width),
        jax.ShapeDtypeStruct((rows, width), jnp.bfloat16),
        arrays + (allowed.astype(jnp.float32),),
        16 * rows * width * arrays[places[1][0]].shape[0],
    )


def attend_backward(arrays, places, width, grad_mixed, allowed):
    rows = grad_mixed.shape[0]
    return kernel_call(
        functools.partial(attend_backward_kernel, places, width),
        tuple(jax.ShapeDtypeStruct(array.shape, array.dtype) for array in arrays),
        arrays + (grad_mixed, allowed.astype(jnp.float32).T),
        40 * rows * width * arrays[places[1][0]].shape[0],
    )


def pick_rows(index, rows):
    return product(index, rows).astype(jnp.bfloat16)


def place_exact(index, rows):
    return jnp.dot(
        index.astype(jnp.float32),
        rows,
        precision=lax.Precision.HIGHEST,
        preferred_element_type=jnp.float32,
    )


def both(partial_rows):
    return partial_rows + swap(partial_rows)


def norm_backward(values, gain, grad):
    grad_values, grad_gain = jax.vjp(norm_rows, values, gain)[1](grad)
    return grad_values, grad_gain


def own_half(rows):
    half = rows.shape[0] // 2
    return jnp.where(lax.axis_index("tensor") == 0, rows[:half], rows[half:])


def in_order(rows):
    other = swap(rows)
    return jnp.where(
        lax.axis_index("tensor") == 0,
        jnp.concatenate([rows, other]),
        jnp.concatenate([other, rows]),
    )


def norm_backward_shared(values, gain, grad):
    grad_values = jax.vjp(lambda rows: norm_rows(rows, gain), values)[1](grad)[0]
    own = own_half(values)
    grad_gain = jax.vjp(lambda scale: norm_rows(own, scale), gain)[1](own_half(grad))[0]
    return grad_values, grad_gain


def tie(*values):
    return lax.optimization_barrier(values)


def low_grad(left, right):
    return product_tn(left, right).astype(jnp.bfloat16)


def low_product(left, right):
    return product(left, right).astype(jnp.bfloat16)


def gelu_exact(values):
    return jax.nn.gelu(values, approximate=False)


def gelu_backward(inner, grad_hidden):
    return jax.vjp(gelu_exact, inner)[1](grad_hidden.astype(jnp.float32))[0].astype(jnp.bfloat16)


def adam_step(master, first, second, grad, clip, fix_one, fix_two, rate):
    grad = grad * clip
    first_new = FIRST_DECAY * first + (1 - FIRST_DECAY) * grad
    second_new = SECOND_DECAY * second + (1 - SECOND_DECAY) * grad * grad
    master_new = master - rate * (
        first_new / fix_one / (jnp.sqrt(second_new / fix_two) + ADAM_EPSILON)
        + WEIGHT_DECAY * master
    )
    return (master_new, first_new, second_new)


def bit_order(turn):
    count = (lax.axis_size("dp") - 1).bit_length()
    order = list(range(count - 1, -1, -1))
    if turn % 2:
        for first in range(0, count - 1, 2):
            order[first], order[first + 1] = order[first + 1], order[first]
    return order


def swap_bit(values, bit):
    pairs = [(group, group ^ (1 << bit)) for group in range(lax.axis_size("dp"))]
    return lax.ppermute(values, "dp", pairs)


class Gather:
    def __init__(self, shard, turn):
        self.held, self.got = shard[None], None
        self.order = bit_order(turn)
        self.bits = []

    def settle(self):
        if self.got is None:
            return
        bit = self.order[len(self.bits)]
        block = self.held.shape[1:]
        above = sum(1 for other in self.bits if other > bit)
        shape = (2**above, 2 ** (len(self.bits) - above)) + block
        held = jnp.stack([self.held.reshape(shape), self.got.reshape(shape)], axis=1)
        self.held, self.got = held.reshape((-1,) + block), None
        self.bits.append(bit)

    def step(self):
        self.settle()
        self.got = swap_bit(self.held, self.order[len(self.bits)])

    def left(self):
        return len(self.order) - len(self.bits) - (self.got is not None)

    def rows(self):
        while self.left():
            self.step()
        self.settle()
        return self.held.reshape(-1, self.held.shape[2])


class Scatter:
    def __init__(self, grads, turn):
        groups = lax.axis_size("dp")
        self.held = grads.reshape((groups, grads.shape[0] // groups, grads.shape[1]))
        self.got = None
        self.order = bit_order(turn)
        self.bits = sorted(self.order, reverse=True)

    def settle(self):
        if self.got is not None:
            held = self.held.astype(jnp.float32) + self.got.astype(jnp.float32)
            self.held, self.got = held.reshape((-1,) + held.shape[2:]), None

    def step(self):
        self.settle()
        bit = self.order.pop()
        above = self.bits.index(bit)
        halves = self.held.reshape((2**above, 2, -1) + self.held.shape[1:])
        self.got = swap_bit(halves[:, 1].astype(jnp.bfloat16), bit)
        self.held = halves[:, 0]
        self.bits.remove(bit)

    def left(self):
        return len(self.order)

    def rows(self):
        while self.left():
            self.step()
        self.settle()
        return self.held[0]


def joined(scatters):
    whole = Scatter(jnp.zeros((lax.axis_size("dp"), 1)), 0)
    for scatter in scatters:
        scatter.settle()
    whole.held = jnp.concatenate([scatter.held for scatter in scatters], axis=2)
    whole.order, whole.bits = list(scatters[0].order), list(scatters[0].bits)
    return whole


def advance(movers):
    for mover in movers:
        if mover.left():
            mover.step()


def meet(value, movers):
    sent = [mover for mover in movers if mover.got is not None]
    tied = tie(value, *[mover.got for mover in sent])
    for mover, got in zip(sent, tied[1:]):
        mover.got = got
    return tied[0]


def flipped(values):
    return jnp.swapaxes(values, -1, -2)


def request_slots(ids, rows_owned):
    owner = ids // rows_owned
    here = jnp.arange(ids.shape[0])
    earlier = here[None, :] < here[:, None]
    same = ids[:, None] == ids[None, :]
    leads = jnp.sum((same & earlier).astype(jnp.int32), axis=1) == 0
    leader = jnp.min(jnp.where(same, here[None, :], ids.shape[0]), axis=1)
    rank = jnp.sum(
        (
            (here[None, :] < leader[:, None])
            & leads[None, :]
            & (owner[:, None] == owner[None, :])
        ).astype(jnp.int32),
        axis=1,
    )
    return owner, rank, leads


def chosen_rows(index, count, dtype=jnp.bfloat16):
    return (index[:, None] == jnp.arange(count)[None, :]).astype(dtype)


def local(
    source_ids,
    target_ids,
    score_places,
    target_labels,
    source_lengths,
    target_lengths,
    pair_order,
    step_count,
    entry_weight,
    entry_first,
    entry_second,
    exit_weight,
    exit_first,
    exit_second,
    expand_weight,
    expand_first,
    expand_second,
    reduce_weight,
    reduce_first,
    reduce_second,
    norm_gains,
    gains_first,
    gains_second,
    token_table,
    table_first,
    table_second,
    place_table,
    place_first,
    place_second,
):
    groups = lax.axis_size("dp")
    parts = lax.axis_size("tensor")
    devices = groups * parts
    group = lax.axis_index("dp")
    part = lax.axis_index("tensor")
    low = jnp.bfloat16
    rows_owned, width = token_table.shape
    half = source_ids.shape[1]
    spot_share = score_places.shape[1]

    share = width // groups
    feature = jnp.arange(width)
    home = (feature // share ^ group) * share + feature % share
    order = home[:, None] == feature[None, :]

    def reordered(values):
        return product(values, order.astype(low))

    def reordered_exact(values):
        return jnp.dot(
            values,
            order.astype(jnp.float32),
            precision=lax.Precision.HIGHEST,
            preferred_element_type=jnp.float32,
        )

    gains = reordered_exact(norm_gains)
    blocks = entry_weight.shape[3]
    entry_low = entry_weight.astype(low)
    leave_low = flipped(exit_weight.astype(low))
    place_low = flipped(place_table.astype(low))
    expand_low = expand_weight.astype(low)
    shrink_low = flipped(reduce_weight.astype(low))
    wide = expand_low.shape[2]

    def beside(*pieces):
        return jnp.concatenate(pieces, axis=1)

    attend_gathers = [
        Gather(beside(entry_low[0, 0], entry_low[0, 1]), 0),
        Gather(beside(entry_low[0, 2], leave_low[0], place_low[0]), 1),
    ]
    late_gathers = [
        Gather(
            beside(entry_low[1, 0], entry_low[1, 1], entry_low[1, 2], leave_low[1], place_low[1]),
            0,
        ),
        Gather(beside(entry_low[2, 0], entry_low[2, 1], entry_low[2, 2], leave_low[2]), 1),
    ]
    advance(attend_gathers)
    feed_weights = [
        lax.all_gather(jnp.stack([expand_low[b], shrink_low[b]]), "dp", axis=1, tiled=True)
        for b in range(2)
    ]

    def pieces_of(values, first, count):
        return [
            values[:, first + b * blocks : first + (b + 1) * blocks] for b in range(count)
        ]

    ids = jnp.concatenate([source_ids[0], target_ids[0]])
    owner, rank, leads = request_slots(ids, rows_owned)
    rounds = jnp.max(rank) // SLOTS + 1
    slots_all = devices * SLOTS
    slot_names = jnp.arange(slots_all)

    def slot_in(turn):
        return jnp.where(rank // SLOTS == turn, owner * SLOTS + rank % SLOTS, -1)

    def requests_in(turn):
        asked = (slot_names[:, None] == slot_in(turn)[None, :]) & leads[None, :]
        return jnp.sum(
            jnp.where(asked, ids[None, :] % rows_owned + 1, 0), axis=1
        ).reshape(devices, SLOTS)

    spots = score_places[0]
    extras = jnp.concatenate(
        [
            spots,
            target_labels[0],
            (spots < target_lengths[0]).astype(jnp.int32),
            rounds[None],
        ]
    )
    message = jnp.concatenate(
        [
            requests_in(0),
            jnp.broadcast_to(extras[None], (devices, extras.shape[0])),
        ],
        axis=1,
    )
    heard = lax.all_to_all(message, EVERY, 0, 0, tiled=True)
    heard = meet(heard, attend_gathers)
    advance(attend_gathers)
    asked_first = heard[:, :SLOTS].reshape(-1) - 1
    spots_all = heard[:, SLOTS : SLOTS + spot_share]
    labels_all = heard[:, SLOTS + spot_share : SLOTS + 2 * spot_share]
    valid_all = heard[:, SLOTS + 2 * spot_share : SLOTS + 3 * spot_share]
    rounds_all = jnp.max(heard[:, -1])
    own_table = token_table.astype(low)

    def picked_rows(asked):
        return product(chosen_rows(asked, rows_owned), own_table).astype(low)

    def answer(sent):
        return lax.all_to_all(
            sent.reshape(devices, SLOTS, width), EVERY, 0, 0, tiled=True
        ).reshape(slots_all, width)

    def looked_up(got, slot):
        return product(chosen_rows(slot, slots_all), got)

    def ask_again(turn):
        return (
            lax.all_to_all(requests_in(turn), EVERY, 0, 0, tiled=True).reshape(-1) - 1
        )

    asked_rows = meet(picked_rows(asked_first), attend_gathers)
    got = answer(asked_rows)
    advance(attend_gathers)
    late_gathers[0].held, late_gathers[1].held = tie(
        meet(late_gathers[0].held, attend_gathers), late_gathers[1].held
    )
    advance(attend_gathers)
    advance(late_gathers)
    got = meet(got, attend_gathers + late_gathers)
    got, feed_weights[0] = tie(got, feed_weights[0])
    advance(late_gathers)
    expand_zero = pick_rows(order.astype(low), feed_weights[0][0])
    shrink_zero = pick_rows(order.astype(low), feed_weights[0][1])
    start = looked_up(got, slot_in(0))
    start = lax.while_loop(
        lambda state: state[0] < rounds_all,
        lambda state: (
            state[0] + 1,
            state[1] + looked_up(answer(picked_rows(ask_again(state[0]))), slot_in(state[0])),
        ),
        (jnp.int32(1), start),
    )[1]
    first_one, first_two = [gather.rows() for gather in attend_gathers]
    value_zero = first_two[:, :blocks]
    leave_zero = first_two[:, blocks : 2 * blocks]
    start = reordered(start.astype(low)).reshape(2, half, width)

    row_places = jnp.concatenate(
        [part * half + jnp.arange(half), (1 - part) * half + jnp.arange(half)]
    )
    spots_group = lax.dynamic_index_in_dim(
        spots_all.reshape(groups, parts, spot_share), group, 0, False
    )
    spots_group = spots_group.reshape(-1)
    encoder_mask = row_places[None, :] < source_lengths[0]
    decoder_mask = (row_places[None, :] <= spots_group[:, None]) & (
        row_places[None, :] < target_lengths[0]
    )
    scored_row = spots_group[:, None] == row_places[None, :]
    heads = ((0, 0), (0, blocks), (1, 0))
    enc_start = start[0] + flipped(first_two[:, 2 * blocks :]).astype(jnp.float32)
    enc_rows = meet(norm_rows(enc_start, gains[0]).astype(low), late_gathers)
    advance(late_gathers)
    enc_rows = spread(enc_rows)
    enc_pair = low_product(enc_rows, first_one)
    enc_arrays = (enc_pair, low_product(enc_rows, value_zero))
    enc_mixed = attend_forward(enc_arrays, heads, blocks, encoder_mask)
    enc_mixed = meet(enc_mixed, late_gathers)
    advance(late_gathers)
    stream = enc_start + collect(product_nt(enc_mixed, leave_zero))

    feed_rows = spread(norm_rows(stream, gains[1]).astype(low))
    feed_inner = product(feed_rows, expand_zero)
    feed_hidden = meet(gelu_exact(feed_inner).astype(low), late_gathers)
    after_feed = stream + collect(product_nt(feed_hidden, shrink_zero))
    memory = norm_rows(after_feed, gains[2]).astype(low)

    split = ((0, 0), (1, 0), (1, blocks))
    memory = spread(meet(memory, late_gathers))
    self_weights, cross_weights = [gather.rows() for gather in late_gathers]
    self_query = self_weights[:, :blocks]
    self_keyval = self_weights[:, blocks : 3 * blocks]
    self_leave_weight = self_weights[:, 3 * blocks : 4 * blocks]
    dec_start = start[1] + flipped(self_weights[:, 4 * blocks :]).astype(jnp.float32)
    target_rows = spread(dec_start)
    dec_source = norm_rows(target_rows, gains[3]).astype(low)
    dec_rows = pick_rows(scored_row.astype(low), dec_source)
    dec_arrays = (low_product(dec_rows, self_query), low_product(dec_source, self_keyval))
    dec_mixed = attend_forward(dec_arrays, split, blocks, decoder_mask)
    after_self = place_exact(scored_row, target_rows) + both(
        product_nt(dec_mixed, self_leave_weight)
    )

    cross_query_weight = cross_weights[:, :blocks]
    cross_keyval_weight = cross_weights[:, blocks : 3 * blocks]
    cross_leave_weight = cross_weights[:, 3 * blocks :]
    cross_rows = norm_rows(after_self, gains[4]).astype(low)
    cross_rows, last_weights = tie(cross_rows, feed_weights[1])
    cross_arrays = (
        low_product(cross_rows, cross_query_weight),
        low_product(memory, cross_keyval_weight),
    )
    cross_mixed = attend_forward(cross_arrays, split, blocks, encoder_mask)
    after_cross = after_self + both(product_nt(cross_mixed, cross_leave_weight))

    after_cross = reordered_exact(after_cross)
    expand_one, shrink_one = last_weights[0], last_weights[1]
    last_rows = norm_rows(after_cross, norm_gains[5]).astype(low)
    last_inner = product(last_rows, expand_one)
    last_hidden = gelu_exact(last_inner).astype(low)
    after_last = after_cross + both(product_nt(last_hidden, shrink_one))
    final = norm_rows(after_last, norm_gains[6]).astype(low)

    picked_group = to_all(own_half(final), "dp")
    picked = in_order(picked_group.reshape(-1, width))

    def cores_first(values):
        return jnp.swapaxes(values.reshape(groups, parts, spot_share), 0, 1).reshape(-1)

    label_row = cores_first(labels_all) - (group * parts + part) * rows_owned
    valid = cores_first(valid_all).astype(jnp.float32)
    count = jnp.sum(valid)
    scored_half = picked.shape[0] // 2
    logits = product_nt(picked, own_table)
    onehot = chosen_rows(label_row, rows_owned, jnp.bool_)
    highest = jnp.max(logits, axis=-1)
    log_here = highest + jnp.log(jnp.sum(jnp.exp(logits - highest[:, None]), axis=-1))
    golden_here = jnp.sum(jnp.where(onehot, logits, 0.0), axis=-1)
    stats = to_all(jnp.stack([log_here, golden_here]))
    top = jnp.max(stats[:, 0], axis=0)
    log_total = top + jnp.log(jnp.sum(jnp.exp(stats[:, 0] - top[None]), axis=0))
    golden = jnp.sum(stats[:, 1], axis=0)
    losses = (log_total - golden) * valid
    mean_loss = jnp.sum(losses) / count
    of_group = (pair_order == group).astype(jnp.float32)
    pair_rows = jnp.sum(
        losses.reshape(parts, groups, spot_share) * of_group[None, :, None], axis=1
    )
    pair_losses = jnp.where(part == 0, pair_rows[0], pair_rows[1])[None]
    probs = jnp.exp(logits - log_total[:, None])
    grad_logits = (
        (probs - onehot.astype(jnp.float32)) * (valid / count)[:, None]
    ).astype(low)
    grad_picked = product(grad_logits, own_table)
    kept = own_half(grad_picked)
    sent = jnp.where(part == 0, grad_picked[scored_half:], grad_picked[:scored_half])
    grad_picked = lax.all_to_all(
        (kept + swap(sent)).astype(low).reshape(groups, spot_share, width),
        "dp",
        0,
        0,
        tiled=True,
    )
    grad_final = in_order(jnp.sum(grad_picked.astype(jnp.float32), axis=0))
    grad_table = product_tn(grad_logits, picked)

    grad_rows, gain_six = norm_backward_shared(after_last, norm_gains[6], grad_final)
    grad_low = grad_rows.astype(low)
    last_grads = [low_grad(grad_low, last_hidden)]
    grad_inner = gelu_backward(last_inner, product(grad_low, shrink_one).astype(low))
    last_grads = lax.psum_scatter(
        jnp.stack([low_grad(last_rows, grad_inner)] + last_grads),
        "dp",
        scatter_dimension=1,
        tiled=True,
    ).astype(jnp.float32)
    grad_values, gain_five = norm_backward_shared(
        after_cross, norm_gains[5], both(product_nt(grad_inner, expand_one))
    )
    grad_rows = reordered_exact(grad_rows + grad_values)

    grad_low = grad_rows.astype(low)
    cross_leave = low_grad(grad_low, cross_mixed)
    grad_mixed = low_product(grad_low, cross_leave_weight)
    grad_query, grad_keyval = attend_backward(
        cross_arrays, split, blocks, grad_mixed, encoder_mask
    )
    cross_scatters = [
        Scatter(beside(low_grad(cross_rows, grad_query), cross_leave), 0),
        Scatter(low_grad(memory, grad_keyval), 1),
    ]
    advance(cross_scatters)
    back_source = product_nt(grad_keyval, cross_keyval_weight)
    back_rows = product_nt(grad_query, cross_query_weight)
    grad_stream, gain_two = norm_backward(after_feed, gains[2], collect(back_source))

    grad_all = spread(grad_stream.astype(low))
    grad_inner = gelu_backward(feed_inner, product(grad_all, shrink_zero).astype(low))
    feed_scatters = [Scatter(low_grad(grad_all, feed_hidden), 0)]
    feed_scatters.append(Scatter(low_grad(feed_rows, grad_inner), 1))
    advance(feed_scatters)
    back = product_nt(grad_inner, expand_zero)
    back, back_rows = tie(back, back_rows)
    grad_values, gain_one = norm_backward(stream, gains[1], collect(back))
    grad_stream = grad_stream + grad_values

    grad_values, gain_four = norm_backward_shared(after_self, gains[4], both(back_rows))
    grad_rows = grad_rows + grad_values
    grad_low = grad_rows.astype(low)
    self_leave = low_grad(grad_low, dec_mixed)
    grad_mixed = low_product(grad_low, self_leave_weight)
    grad_query, grad_keyval = attend_backward(
        dec_arrays, split, blocks, grad_mixed, decoder_mask
    )
    self_scatters = [
        Scatter(beside(low_grad(dec_rows, grad_query), self_leave), 0),
        Scatter(low_grad(dec_source, grad_keyval), 1),
    ]
    advance(self_scatters)
    back_source = product_nt(grad_keyval, self_keyval) + place_exact(
        scored_row.T, product_nt(grad_query, self_query)
    )
    grad_decoded, gain_three = norm_backward(dec_start, gains[3], collect(back_source))
    grad_decoded = grad_decoded + place_exact(scored_row[:, :half].T, grad_rows)
    start_decoded = grad_decoded.astype(low)

    grad_all = spread(grad_stream.astype(low))
    grad_mixed = low_product(grad_all, leave_zero)
    first_scatters = [
        Scatter(beside(low_grad(grad_all, enc_mixed), flipped(start_decoded)), 0)
    ]
    advance(first_scatters)
    grad_pair, grad_value = attend_backward(enc_arrays, heads, blocks, grad_mixed, encoder_mask)
    grad_pair = meet(grad_pair, cross_scatters + feed_scatters)
    early = [joined([cross_scatters[b], feed_scatters[b]]) for b in range(2)]
    advance(early)
    back = product_nt(grad_pair, first_one) + product_nt(grad_value, value_zero)
    first_scatters += [
        Scatter(low_grad(enc_rows, grad_pair), 1),
        Scatter(low_grad(enc_rows, grad_value), 0),
    ]
    advance(first_scatters[1:])
    grad_values, gain_zero = norm_backward(enc_start, gains[0], collect(back))
    start_stream = (grad_stream + grad_values).astype(low)
    place_scatter = Scatter(flipped(start_stream), 1)
    advance([place_scatter])

    start_rows = reordered(jnp.concatenate([start_stream, start_decoded])).astype(low)

    def returned(slot):
        return answer(product_tn(chosen_rows(slot, slots_all), start_rows).astype(low))

    def placed(asked, got):
        return product_tn(chosen_rows(asked, rows_owned), got)

    got = returned(slot_in(0))
    got = meet(got, early)
    got = meet(got, self_scatters + first_scatters + [place_scatter])
    got, last_grads = tie(got, last_grads)
    late = [
        joined([self_scatters[0], first_scatters[0], first_scatters[2]]),
        joined([self_scatters[1], first_scatters[1], place_scatter]),
    ]
    advance(early)
    advance(late)
    table_grad = grad_table + placed(asked_first, got)
    table_grad = lax.while_loop(
        lambda state: state[0] < rounds_all,
        lambda state: (
            state[0] + 1,
            state[1] + placed(ask_again(state[0]), returned(slot_in(state[0]))),
        ),
        (jnp.int32(1), table_grad),
    )[1]
    table_grad = meet(table_grad, early + late)
    advance(early)
    advance(late)
    gain_partial = jnp.concatenate(
        [
            reordered_exact(jnp.stack([gain_zero, gain_one, gain_two, gain_three, gain_four])),
            jnp.stack([gain_five, gain_six]),
        ]
    )
    gain_partial, table_grad = tie(gain_partial, table_grad)
    gain_own = jnp.sum(
        lax.all_to_all(gain_partial.reshape(devices, -1), EVERY, 0, 0, tiled=True), axis=0
    )
    squares = jnp.sum(table_grad * table_grad)
    squares, gain_own = tie(squares, gain_own)
    squares = meet(squares, early + late)
    advance(late)
    early_rows = [scatter.rows() for scatter in early]
    late_rows = [scatter.rows() for scatter in late]
    stream_place = late_rows[1][:, 4 * blocks :]
    def attention_grads(outer, keyval):
        return [outer[:, :blocks], keyval[:, :blocks], keyval[:, blocks:], outer[:, blocks:]]

    cross_pieces = attention_grads(*[rows[:, : 2 * blocks] for rows in early_rows])
    shrink_rows, expand_rows = [rows[:, 2 * blocks :] for rows in early_rows]
    self_pieces = attention_grads(*[rows[:, : 2 * blocks] for rows in late_rows])
    first_leave, decoded_place, first_value = jnp.split(
        late_rows[0][:, 2 * blocks :], [blocks, blocks + half], axis=1
    )
    first_pieces = pieces_of(late_rows[1], 2 * blocks, 2) + [first_value, first_leave]
    entry_grad = jnp.stack(
        [jnp.stack(pieces[:3]) for pieces in (first_pieces, self_pieces, cross_pieces)]
    )
    leave_grad = flipped(jnp.stack([first_pieces[3], self_pieces[3], cross_pieces[3]]))
    expand_grad = jnp.stack([expand_rows, last_grads[0]])
    shrink_grad = flipped(jnp.stack([shrink_rows, last_grads[1]]))
    place_grad = flipped(jnp.stack([stream_place, decoded_place]))
    squares = squares + jnp.sum(gain_own * gain_own)
    for grad in (entry_grad, leave_grad, expand_grad, shrink_grad, place_grad):
        squares = squares + jnp.sum(grad * grad)
    last_words = to_all(jnp.concatenate([gain_own, squares[None]]))
    gain_grad = last_words[:, :-1].reshape(norm_gains.shape)
    gradient_norm = jnp.sqrt(jnp.sum(last_words[:, -1]))
    clip = jnp.minimum(1.0, MAX_NORM / (gradient_norm + 1e-06))
    steps = step_count[0].astype(jnp.float32)
    fix_one = 1 - FIRST_DECAY**steps
    fix_two = 1 - SECOND_DECAY**steps
    masters = (
        entry_weight,
        exit_weight,
        expand_weight,
        reduce_weight,
        norm_gains,
        token_table,
        place_table,
    )
    firsts = (
        entry_first,
        exit_first,
        expand_first,
        reduce_first,
        gains_first,
        table_first,
        place_first,
    )
    seconds = (
        entry_second,
        exit_second,
        expand_second,
        reduce_second,
        gains_second,
        table_second,
        place_second,
    )
    grads = (entry_grad, leave_grad, expand_grad, shrink_grad, gain_grad, table_grad, place_grad)
    rates = (LEARN_RATE, LEARN_RATE, LEARN_RATE, LEARN_RATE, GAIN_RATE, LEARN_RATE, LEARN_RATE)
    results = [mean_loss, gradient_norm, pair_losses]
    for master, first, second, grad, rate in zip(masters, firsts, seconds, grads, rates):
        results.extend(adam_step(master, first, second, grad, clip, fix_one, fix_two, rate))
    return tuple(results)


def solution(mesh):
    return jax.shard_map(
        local,
        mesh=mesh,
        in_specs=(
            P("dp", "tensor"),
            P("dp", "tensor"),
            P("dp", "tensor"),
            P("dp", "tensor"),
            P("dp"),
            P("dp"),
            P(),
            P(),
            P(None, None, "dp", "tensor"),
            P(None, None, "dp", "tensor"),
            P(None, None, "dp", "tensor"),
            P(None, "tensor", "dp"),
            P(None, "tensor", "dp"),
            P(None, "tensor", "dp"),
            P(None, "dp", "tensor"),
            P(None, "dp", "tensor"),
            P(None, "dp", "tensor"),
            P(None, "tensor", "dp"),
            P(None, "tensor", "dp"),
            P(None, "tensor", "dp"),
            P(),
            P(),
            P(),
            P(("dp", "tensor"), None),
            P(("dp", "tensor"), None),
            P(("dp", "tensor"), None),
            P(None, "tensor", "dp"),
            P(None, "tensor", "dp"),
            P(None, "tensor", "dp"),
        ),
        out_specs=(
            P(),
            P(),
            P("dp", "tensor"),
            P(None, None, "dp", "tensor"),
            P(None, None, "dp", "tensor"),
            P(None, None, "dp", "tensor"),
            P(None, "tensor", "dp"),
            P(None, "tensor", "dp"),
            P(None, "tensor", "dp"),
            P(None, "dp", "tensor"),
            P(None, "dp", "tensor"),
            P(None, "dp", "tensor"),
            P(None, "tensor", "dp"),
            P(None, "tensor", "dp"),
            P(None, "tensor", "dp"),
            P(),
            P(),
            P(),
            P(("dp", "tensor"), None),
            P(("dp", "tensor"), None),
            P(("dp", "tensor"), None),
            P(None, "tensor", "dp"),
            P(None, "tensor", "dp"),
            P(None, "tensor", "dp"),
        ),
        check_vma=False,
    )
```
